256 devices in a mesh: row: 32 (over z, y), col: 8 (over x, core).
Axes of the slice: x: 4, y: 4, z: 8, core: 2. Of those that a mesh axis runs over, the one named last changes fastest.
Arguments:
- momentum: float32 [5120, 9216], P('row', 'col'), may hold values from -300 to 300
- gradient: bfloat16 [5120, 9216], P('row', 'col'), may hold values from -300 to 300
Outputs:
- new_momentum: float32 [5120, 9216], P('row', 'col')
- update: float32 [5120, 9216], P('row', 'col')
The draws below stay inside these ranges and needn't reach their ends.
All inputs are finite; a program needn't handle non-finite values.
Results may differ from the reference program's by a relative error of at most 0.0004.
The reference program's roundings to bfloat16 on the way count: a program that leaves them out, or rounds other values in their place, can miss the bound.
Values may be sent and summed in bfloat16 or wider, within the bound.
A program may use at most 128 MiB of HBM per device.

```python
import math
import jax
import jax.numpy as jnp

M = 5120
N = 9216


def ramp_profile():
    row_ids = jnp.arange(M, dtype=jnp.float32)
    col_ids = jnp.arange(N, dtype=jnp.float32)
    return jnp.sqrt(1.0 + row_ids / M)[:, None] * jnp.sqrt(1.0 + 0.5 * col_ids / N)[None, :]


def draw_momentum(key, part):
    key = jax.random.fold_in(key, 7)
    first = jax.random.fold_in(key, 0)
    values = jnp.clip(jax.random.normal(first, (M, N), jnp.float32), -5.0, 5.0)
    return (values * ramp_profile()).astype(jnp.float32)


def draw_gradient(key, part):
    key = jax.random.fold_in(key, 11)
    first = jax.random.fold_in(key, 0)
    values = jnp.clip(jax.random.normal(first, (M, N), jnp.float32), -5.0, 5.0)
    return (values * ramp_profile()).astype(jnp.bfloat16)


def setup_inputs(seed: int = 0) -> dict:
    seeds = jax.random.split(jax.random.key(seed), 3)
    return {
        "momentum": draw_momentum(jax.random.fold_in(seeds[2], 71), 0),
        "gradient": draw_gradient(jax.random.fold_in(seeds[2], 71), 0),
    }


decay_rate = 0.95
linear_coef = 3.4445
cubic_coef = -4.775
quintic_coef = 2.0315
norm_eps = 1e-07

def reference(momentum, gradient):
    new_momentum = decay_rate * momentum + gradient.astype(jnp.float32)
    iterate = new_momentum.astype(jnp.bfloat16)
    wide_iterate = iterate.astype(jnp.float32)
    sumsq = jnp.sum(wide_iterate * wide_iterate)
    factor = math.sqrt(M) / (3.0 * (jnp.sqrt(sumsq) + norm_eps))
    gram_full = jnp.dot(iterate, iterate.T, preferred_element_type=jnp.float32)
    gram_bf = gram_full.astype(jnp.bfloat16)
    square = jnp.dot(gram_bf, gram_bf, preferred_element_type=jnp.float32)
    polynom = (cubic_coef * factor * factor * gram_bf.astype(jnp.float32) + quintic_coef * factor ** 4 * square).astype(jnp.bfloat16)
    product = jnp.dot(polynom, iterate, preferred_element_type=jnp.float32)
    update = math.sqrt(N) * factor * (linear_coef * wide_iterate + product)
    return (new_momentum, update)
```

```python
import math

import jax
import jax.numpy as jnp
from jax import lax
from jax.sharding import PartitionSpec as P

decay_rate = 0.95
linear_coef = 3.4445
cubic_coef = -4.775
quintic_coef = 2.0315
norm_eps = 1e-07

Y = 4
Z = 8


def local(momentum, gradient):
    new_momentum = decay_rate * momentum + gradient.astype(jnp.float32)
    iterate = new_momentum.astype(jnp.bfloat16)
    wide_iterate = iterate.astype(jnp.float32)
    rows_here, cols_here = iterate.shape
    width_rows = rows_here * lax.axis_size("row")
    width_cols = cols_here * lax.axis_size("col")
    along_y = [[z * Y + y for y in range(Y)] for z in range(Z)]
    along_z = [[z * Y + y for z in range(Z)] for y in range(Y)]
    norm_total = lax.psum(jnp.sum(wide_iterate * wide_iterate), ("row", "col"))
    rows_z = lax.all_gather(iterate, "row", axis=0, tiled=True, axis_index_groups=along_y)
    rows_y = lax.all_gather(iterate, "row", axis=0, tiled=True, axis_index_groups=along_z)
    partial_gram = lax.dot_general(
        rows_y, rows_z, (((1,), (1,)), ((), ())), preferred_element_type=jnp.float32
    )
    tile = lax.psum_scatter(partial_gram, "col", scatter_dimension=0, tiled=True)
    tile_bf = tile.astype(jnp.bfloat16)
    panel = lax.all_gather(tile_bf, "row", axis=1, tiled=True, axis_index_groups=along_z)
    column = lax.all_gather(tile_bf, "row", axis=0, axis_index_groups=along_y)
    column = lax.all_gather(column, "col", axis=0)
    column = column.reshape(width_rows, tile.shape[1])
    square = jnp.dot(panel, column, preferred_element_type=jnp.float32)
    factor = math.sqrt(width_rows) / (3.0 * (jnp.sqrt(norm_total) + norm_eps))
    polynom = (
        cubic_coef * factor * factor * tile_bf.astype(jnp.float32)
        + quintic_coef * factor**4 * square
    ).astype(jnp.bfloat16)
    wide_polynom = lax.all_gather(polynom, "col", axis=0, tiled=True)
    partial_product = lax.dot_general(
        wide_polynom, rows_y, (((0,), (0,)), ((), ())), preferred_element_type=jnp.float32
    )
    product = lax.psum_scatter(
        partial_product, "row", scatter_dimension=0, tiled=True, axis_index_groups=along_y
    )
    update = math.sqrt(width_cols) * factor * (linear_coef * wide_iterate + product)
    return (new_momentum, update)


def solution(mesh):
    placed = (P("row", "col"), P("row", "col"))
    return jax.shard_map(
        local,
        mesh=mesh,
        in_specs=placed,
        out_specs=(P("row", "col"), P("row", "col")),
        check_vma=False,
    )
```

```python
import math

import jax
import jax.numpy as jnp
from jax import lax
from jax.experimental import pallas as pl
from jax.experimental.pallas import tpu as pltpu
from jax.sharding import PartitionSpec as P

decay_rate = 0.95
linear_coef = 3.4445
cubic_coef = -4.775
quintic_coef = 2.0315
norm_eps = 1e-07

X, Y, Z = 4, 4, 8
ROWS, COLS = 160, 1152
HALF = ROWS // 2
WIDE = Y * ROWS
TILES = 3
TILE = COLS // TILES
FULL_ROWS = ROWS * Y * Z
FULL_COLS = COLS * X * 2
NT = (((1,), (1,)), ((), ()))
TN = (((0,), (0,)), ((), ()))
F32 = jnp.float32
BF16 = jnp.bfloat16


def wrap(value, size):
    return lax.rem(value + size, size)


def remote(src, dst, send_sem, recv_sem, device):
    return pltpu.make_async_remote_copy(
        src_ref=src,
        dst_ref=dst,
        send_sem=send_sem,
        recv_sem=recv_sem,
        device_id=device,
        device_id_type=pl.DeviceIdType.MESH,
    )


class Ring:
    def __init__(self, size, position, device, region, last, send_sems, recv_sems):
        self.size, self.position, self.device = size, position, device
        self.region, self.last = region, last
        self.send_sems, self.recv_sems = send_sems, recv_sems

    def steps(self, way, piece):
        return self.size // 2 - (0 if self.last[piece] == way else 1)

    def copy(self, way, step, piece, block):
        sign = 1 - 2 * way
        place = self.region(block, piece)
        return remote(
            place,
            place,
            self.send_sems.at[way, step, piece],
            self.recv_sems.at[way, step, piece],
            self.device(wrap(self.position + sign, self.size)),
        )

    def send(self, way, step, piece):
        sign = 1 - 2 * way
        self.copy(way, step, piece, wrap(self.position - sign * step, self.size)).start()

    def start(self, piece):
        for way in (0, 1):
            self.send(way, 0, piece)

    def recv(self, way, step, piece):
        if step >= self.steps(way, piece):
            return
        sign = 1 - 2 * way
        self.copy(way, step, piece, wrap(self.position - sign * (step + 1), self.size)).wait_recv()
        if step + 1 < self.steps(way, piece):
            self.send(way, step + 1, piece)

    def finish(self):
        for way in (0, 1):
            for piece in range(len(self.last)):
                for step in range(self.steps(way, piece)):
                    sign = 1 - 2 * way
                    self.copy(way, step, piece, wrap(self.position - sign * step, self.size)).wait_send()


OFFSETS = (0, 1, -1, 2, -2, 3, -3, 4)


def kernel(
    iterate,
    product,
    factor_out,
    xa, xb, part, sibling_part, relay, last_part, gj, gall, pb, up, y_relay, y_last,
    square, ss_z, ss_y, ss_x, ss_c,
    zr_s, zr_r, yr_s, yr_r, sp_s, sp_r, rl_s, rl_r, lp_s, lp_r,
    gz_s, gz_r, gx0_s, gx0_r, gy0_s, gy0_r, gy1_s, gy1_r, gx1_s, gx1_r, gs_s, gs_r,
    pr_s, pr_r, ps_s, ps_r, ssy_s, ssy_r, ssx_s, ssx_r, ssc_s, ssc_r,
    ur_s, ur_r, ul_s, ul_r,
):
    row, col = lax.axis_index("row"), lax.axis_index("col")
    z, y = lax.div(row, Y), lax.rem(row, Y)
    x, core = lax.div(col, 2), lax.rem(col, 2)
    other = 1 - core

    def at_z(p):
        return (p * Y + y, col)

    def at_y(p):
        return (z * Y + p, col)

    def at_x(p):
        return (row, p * 2 + core)

    sibling = (row, x * 2 + other)

    barrier = pltpu.get_barrier_semaphore()
    partners = [at_z(wrap(z + 1, Z)), at_z(wrap(z - 1, Z)), sibling]
    partners += [at_y(wrap(y + d, Y)) for d in (1, 2, 3)]
    partners += [at_x(wrap(x + d, X)) for d in (1, 2, 3)]
    for partner in partners:
        pl.semaphore_signal(barrier, inc=1, device_id=partner, device_id_type=pl.DeviceIdType.MESH)
    xb[z] = iterate[...]
    xa[y] = iterate[...]
    pl.semaphore_wait(barrier, len(partners))

    zr = Ring(Z, z, at_z, lambda b, p: xb.at[b, pl.ds(p * HALF, HALF)], (0, 1), zr_s, zr_r)
    yr = Ring(Y, y, at_y, lambda b, p: xa.at[b, pl.ds(p * HALF, HALF)], (0, 1), yr_s, yr_r)
    for way, piece in ((0, 0), (1, 1), (0, 1), (1, 0)):
        zr.send(way, 0, piece)
        yr.send(way, 0, piece)

    def z_of(event):
        return wrap(z + OFFSETS[event], Z)

    def sibling_copy(there):
        return remote(
            part.at[there, other], sibling_part.at[there], sp_s.at[there], sp_r.at[there], sibling
        )

    def form(event):
        there = z_of(event)
        block = xb[there]
        part[there] = lax.dot_general(
            block, xa[...].reshape(WIDE, COLS), NT, preferred_element_type=F32
        ).reshape(2, HALF, WIDE)
        sibling_copy(there).start()
        wide = block.astype(F32)
        ss_z[there] = jnp.broadcast_to(jnp.sum(wide * wide, keepdims=True), (8, 128))

    def role_of(there):
        return wrap(x - lax.div(there, 2), X)

    def relay_copy(there, side):
        place = pl.ds(side * (HALF // 2), HALF // 2)
        return remote(
            part.at[there, core, place],
            relay.at[there],
            rl_s.at[there, side],
            rl_r.at[there],
            at_x(wrap(x - 1 + 2 * side, X)),
        )

    def last_copy(there, role):
        side = lax.div(role, 2)
        half = lax.rem(there, 2)
        return remote(
            part.at[there, core],
            last_part.at[half, side],
            lp_s.at[there],
            lp_r.at[half, side],
            at_x(wrap(x + role - 2, X)),
        )

    def join(event):
        there = z_of(event)
        sibling_copy(there).wait_recv()
        part[there, core] = part[there, core] + sibling_part[there]

        @pl.when(role_of(there) == 2)
        def _():
            relay_copy(there, 0).start()
            relay_copy(there, 1).start()

    def pass_on(event):
        there = z_of(event)
        role = role_of(there)

        @pl.when(lax.rem(role, 2) == 1)
        def _():
            relay_copy(there, 0).wait_recv()
            place = pl.ds(pl.multiple_of(lax.div(role, 2) * (HALF // 2), 8), HALF // 2)
            part[there, core, place] = part[there, core, place] + relay[there]
            last_copy(there, role).start()

    def z_step(step):
        for way, piece in ((0, 0), (1, 1), (0, 1), (1, 0)):
            zr.recv(way, step, piece)

    z_step(0)
    for step in (0, 1):
        for way, piece in ((0, 0), (1, 1), (0, 1), (1, 0)):
            yr.recv(way, step, piece)
    form(0)
    form(1)
    form(2)
    join(0)
    join(1)
    join(2)
    z_step(1)
    form(3)
    form(4)
    pass_on(0)
    pass_on(1)
    pass_on(2)
    join(3)
    join(4)
    z_step(2)
    form(5)
    form(6)
    pass_on(3)
    pass_on(4)
    join(5)
    join(6)
    z_step(3)
    form(7)
    pass_on(5)
    pass_on(6)
    join(7)
    pass_on(7)

    def small(refs, slot, send_sems, recv_sems, index, device):
        return remote(refs.at[slot], refs.at[slot], send_sems.at[index], recv_sems.at[index], device)

    total = ss_z[0]
    for k in range(1, Z):
        total = total + ss_z[k]
    ss_y[y] = total
    for d in (1, 2, 3):
        small(ss_y, y, ssy_s, ssy_r, d - 1, at_y(wrap(y + d, Y))).start()

    gz = Ring(Z, z, at_z, lambda b, p: gj.at[b, p], (0, 1), gz_s, gz_r)
    cut = ((0, 48), (48, 32))
    gx0 = Ring(X, x, at_x, lambda b, p: gall.at[b, 0, y, core, pl.ds(*cut[p])], (0, 1), gx0_s, gx0_r)
    gy0 = Ring(Y, y, at_y, lambda b, p: gall.at[wrap(x + p, X), 0, b, core], (0, 0, 1, 1), gy0_s, gy0_r)
    gy1 = Ring(Y, y, at_y, lambda b, p: gall.at[x, 1, b, core, pl.ds(*cut[p])], (0, 1), gy1_s, gy1_r)
    gx1 = Ring(X, x, at_x, lambda b, p: gall.at[b, 1, wrap(y + p, Y), core], (0, 0, 1, 1), gx1_s, gx1_r)

    def last_wait(half, side):
        there = 2 * x + half
        remote(
            part.at[there, core], last_part.at[half, side], lp_s.at[there], lp_r.at[half, side], sibling
        ).wait_recv()

    def settle(half):
        last_wait(half, 0)
        last_wait(half, 1)
        tile = (part[2 * x + half, core] + last_part[half, 0] + last_part[half, 1]).astype(BF16)
        gj[z, half] = tile
        gall[x, half, y, core] = tile

    settle(0)
    gx0.start(0)
    gx0.start(1)
    gz.start(0)
    gy0.start(0)
    settle(1)
    gy1.start(0)
    gy1.start(1)
    gz.start(1)
    gx1.start(0)

    for d in (1, 2, 3):
        small(ss_y, wrap(y - d, Y), ssy_s, ssy_r, d - 1, sibling).wait_recv()
    ss_x[x] = ss_y[0] + ss_y[1] + ss_y[2] + ss_y[3]
    for d in (1, 2, 3):
        small(ss_x, x, ssx_s, ssx_r, d - 1, at_x(wrap(x + d, X))).start()

    four = ((0, 0), (1, 1), (0, 1), (1, 0))

    def both(ring, step, pieces):
        for piece in pieces:
            ring.recv(0, step, piece)
            ring.recv(1, step, piece)

    def share(half, index, core_):
        if half == 0:
            place = gall.at[:, 0, wrap(y + index, Y), core_]
        else:
            place = gall.at[wrap(x + index, X), 1, :, core_]
        return remote(place, place, gs_s.at[half, index], gs_r.at[half, index], sibling)

    for way, piece in four:
        gx0.recv(way, 0, piece)
    gy0.start(1)
    gy0.start(3)
    for way, piece in four:
        gy1.recv(way, 0, piece)
    gx1.start(1)
    gx1.start(3)
    both(gz, 0, (0, 1))
    for way, piece in four:
        gx0.recv(way, 1, piece)
    gy0.start(2)
    for way, piece in four:
        gy1.recv(way, 1, piece)
    gx1.start(2)
    share(0, 0, core).start()
    share(1, 0, core).start()

    for d in (1, 2, 3):
        small(ss_x, wrap(x - d, X), ssx_s, ssx_r, d - 1, sibling).wait_recv()
    ss_c[core] = ss_x[0] + ss_x[1] + ss_x[2] + ss_x[3]
    small(ss_c, core, ssc_s, ssc_r, 0, sibling).start()

    both(gy0, 0, (0,))
    both(gx1, 0, (0,))
    both(gz, 1, (0, 1))
    both(gy0, 0, (1, 3))
    both(gx1, 0, (1, 3))
    both(gz, 2, (0, 1))
    both(gy0, 0, (2,))
    both(gx1, 0, (2,))
    for index in (1, 3):
        share(0, index, core).start()
        share(1, index, core).start()
    both(gz, 3, (0, 1))
    both(gy0, 1, (0, 1, 2, 3))
    both(gx1, 1, (0, 1, 2, 3))
    share(0, 2, core).start()
    share(1, 2, core).start()
    small(ss_c, other, ssc_s, ssc_r, 0, sibling).wait_recv()
    norm_total = (ss_c[0] + ss_c[1])[0:1, 0:1]
    factor = math.sqrt(FULL_ROWS) / (3.0 * (jnp.sqrt(norm_total) + norm_eps))
    factor_out[...] = jnp.broadcast_to(factor, (8, 128))
    for index in (0, 1, 3, 2):
        share(0, index, other).wait_recv()
        share(1, index, other).wait_recv()

    square[...] = jnp.zeros_like(square)

    @pl.loop(0, Z)
    def _(there):
        square[...] += jnp.dot(
            gj[there].reshape(ROWS, WIDE),
            gall[lax.div(there, 2), lax.rem(there, 2)].reshape(WIDE, WIDE),
            preferred_element_type=F32,
        )

    pr = Ring(X, x, at_x, lambda b, p: pb.at[b, p, core], (0, 1), pr_s, pr_r)
    for half in (0, 1):
        gram = gj[z, half].astype(F32)
        tile = (
            cubic_coef * factor * factor * gram
            + quintic_coef * (factor * factor) * (factor * factor) * square[pl.ds(half * HALF, HALF)]
        )
        pb[x, half, core] = tile.astype(BF16)
        pr.start(half)

    def share_p(index, core_):
        place = pb.at[wrap(x + index, X), :, core_]
        return remote(place, place, ps_s.at[index], ps_r.at[index], sibling)

    share_p(0, core).start()
    for way, piece in four:
        pr.recv(way, 0, piece)
    share_p(1, core).start()
    share_p(3, core).start()
    for way, piece in four:
        pr.recv(way, 1, piece)
    share_p(2, core).start()
    for index in (0, 1, 3, 2):
        share_p(index, other).wait_recv()

    def y_relay_copy(tile, side):
        return remote(
            up.at[tile, wrap(y + 2, Y), pl.ds(side * HALF, HALF)],
            y_relay.at[tile, side],
            ur_s.at[tile, side],
            ur_r.at[tile, side],
            at_y(wrap(y + 1 - 2 * side, Y)),
        )

    def y_last_copy(tile, side, half):
        return remote(
            up.at[tile, wrap(y + 1 - 2 * side, Y), pl.ds(half * HALF, HALF)],
            y_last.at[tile, side, pl.ds(half * HALF, HALF)],
            ul_s.at[tile, side, half],
            ul_r.at[tile, side, half],
            at_y(wrap(y + 1 - 2 * side, Y)),
        )

    def add_relay(tile):
        for side in (0, 1):
            y_relay_copy(tile, side).wait_recv()
            near = wrap(y + 1 - 2 * side, Y)
            place = pl.ds(side * HALF, HALF)
            up[tile, near, place] = up[tile, near, place] + y_relay[tile, side]
            y_last_copy(tile, side, side).start()

    for tile in range(TILES):
        up[tile] = lax.dot_general(
            pb[...].reshape(Z * ROWS, WIDE),
            xb[:, :, pl.ds(tile * TILE, TILE)].reshape(Z * ROWS, TILE),
            TN,
            preferred_element_type=F32,
        ).reshape(Y, ROWS, TILE)
        for side in (0, 1):
            y_relay_copy(tile, side).start()
        for side in (0, 1):
            y_last_copy(tile, side, 1 - side).start()
    for tile in range(TILES):
        add_relay(tile)
    for tile in range(TILES):
        for side in (0, 1):
            for half in (0, 1):
                y_last_copy(tile, side, half).wait_recv()
        product[:, pl.ds(tile * TILE, TILE)] = up[tile, y] + y_last[tile, 0] + y_last[tile, 1]

    for ring in (zr, yr, gz, gx0, gy0, gy1, gx1, pr):
        ring.finish()
    for event in range(Z):
        there = z_of(event)
        sibling_copy(there).wait_send()
        role = role_of(there)

        @pl.when(role == 2)
        def _():
            relay_copy(there, 0).wait_send()
            relay_copy(there, 1).wait_send()

        @pl.when(lax.rem(role, 2) == 1)
        def _():
            last_copy(there, role).wait_send()

    for d in (1, 2, 3):
        small(ss_y, y, ssy_s, ssy_r, d - 1, sibling).wait_send()
        small(ss_x, x, ssx_s, ssx_r, d - 1, sibling).wait_send()
    small(ss_c, core, ssc_s, ssc_r, 0, sibling).wait_send()
    for index in range(4):
        share(0, index, core).wait_send()
        share(1, index, core).wait_send()
        share_p(index, core).wait_send()
    for tile in range(TILES):
        for side in (0, 1):
            y_relay_copy(tile, side).wait_send()
            for half in (0, 1):
                y_last_copy(tile, side, half).wait_send()


def dma(*shape):
    return pltpu.SemaphoreType.DMA(shape)


def twice(*shape):
    return [dma(*shape), dma(*shape)]


def fused(iterate):
    vmem = pl.BlockSpec(memory_space=pltpu.VMEM)
    return pl.pallas_call(
        kernel,
        out_shape=(
            jax.ShapeDtypeStruct((ROWS, COLS), F32),
            jax.ShapeDtypeStruct((8, 128), F32),
        ),
        in_specs=[vmem],
        out_specs=(vmem, vmem),
        scratch_shapes=[
            pltpu.VMEM((Y, ROWS, COLS), BF16),
            pltpu.VMEM((Z, ROWS, COLS), BF16),
            pltpu.VMEM((Z, 2, HALF, WIDE), F32),
            pltpu.VMEM((Z, HALF, WIDE), F32),
            pltpu.VMEM((Z, HALF // 2, WIDE), F32),
            pltpu.VMEM((2, 2, HALF, WIDE), F32),
            pltpu.VMEM((Z, 2, HALF, WIDE), BF16),
            pltpu.VMEM((X, 2, Y, 2, HALF, WIDE), BF16),
            pltpu.VMEM((X, 2, 2, HALF, WIDE), BF16),
            pltpu.VMEM((TILES, Y, ROWS, TILE), F32),
            pltpu.VMEM((TILES, 2, HALF, TILE), F32),
            pltpu.VMEM((TILES, 2, ROWS, TILE), F32),
            pltpu.VMEM((ROWS, WIDE), F32),
            pltpu.VMEM((Z, 8, 128), F32),
            pltpu.VMEM((Y, 8, 128), F32),
            pltpu.VMEM((X, 8, 128), F32),
            pltpu.VMEM((2, 8, 128), F32),
            *twice(2, 4, 2),
            *twice(2, 2, 2),
            *twice(Z),
            dma(Z, 2), dma(Z),
            dma(Z), dma(2, 2),
            *twice(2, 4, 2),
            *twice(2, 2, 2),
            *twice(2, 2, 4),
            *twice(2, 2, 2),
            *twice(2, 2, 4),
            *twice(2, 4),
            *twice(2, 2, 2),
            *twice(4),
            *twice(3),
            *twice(3),
            *twice(1),
            *twice(TILES, 2),
            *twice(TILES, 2, 2),
        ],
        compiler_params=pltpu.CompilerParams(
            collective_id=0, has_side_effects=True, vmem_limit_bytes=56 * 1024 * 1024
        ),
    )(iterate)


def local(momentum, gradient):
    new_momentum = decay_rate * momentum + gradient.astype(F32)
    iterate = new_momentum.astype(BF16)
    product, factor = fused(iterate)
    update = math.sqrt(FULL_COLS) * factor[0, 0] * (linear_coef * iterate.astype(F32) + product)
    return (new_momentum, update)


def solution(mesh):
    placed = (P("row", "col"), P("row", "col"))
    return jax.shard_map(
        local,
        mesh=mesh,
        in_specs=placed,
        out_specs=(P("row", "col"), P("row", "col")),
        check_vma=False,
    )
```

```python
import math

import jax
import jax.numpy as jnp
from jax import lax
from jax.experimental import pallas as pl
from jax.experimental.pallas import tpu as pltpu
from jax.sharding import PartitionSpec as P

decay_rate = 0.95
linear_coef = 3.4445
cubic_coef = -4.775
quintic_coef = 2.0315
norm_eps = 1e-07

X, Y, Z = 4, 4, 8
ROWS, COLS = 160, 1152
HALF = ROWS // 2
WIDE = Y * ROWS
TILES = 3
TILE = COLS // TILES
FULL_ROWS = ROWS * Y * Z
FULL_COLS = COLS * X * 2
NT = (((1,), (1,)), ((), ()))
TN = (((0,), (0,)), ((), ()))
F32 = jnp.float32
BF16 = jnp.bfloat16


def wrap(value, size):
    return lax.rem(value + size, size)


def remote(src, dst, send_sem, recv_sem, device):
    return pltpu.make_async_remote_copy(
        src_ref=src,
        dst_ref=dst,
        send_sem=send_sem,
        recv_sem=recv_sem,
        device_id=device,
        device_id_type=pl.DeviceIdType.MESH,
    )


class Ring:
    def __init__(self, size, position, device, region, last, send_sems, recv_sems):
        self.size, self.position, self.device = size, position, device
        self.region, self.last = region, last
        self.send_sems, self.recv_sems = send_sems, recv_sems

    def steps(self, way, piece):
        return self.size // 2 - (0 if self.last[piece] == way else 1)

    def copy(self, way, step, piece, block):
        sign = 1 - 2 * way
        place = self.region(block, piece)
        return remote(
            place,
            place,
            self.send_sems.at[way, step, piece],
            self.recv_sems.at[way, step, piece],
            self.device(wrap(self.position + sign, self.size)),
        )

    def send(self, way, step, piece):
        sign = 1 - 2 * way
        self.copy(way, step, piece, wrap(self.position - sign * step, self.size)).start()

    def start(self, piece):
        for way in (0, 1):
            self.send(way, 0, piece)

    def recv(self, way, step, piece):
        if step >= self.steps(way, piece):
            return
        sign = 1 - 2 * way
        self.copy(way, step, piece, wrap(self.position - sign * (step + 1), self.size)).wait_recv()
        if step + 1 < self.steps(way, piece):
            self.send(way, step + 1, piece)

    def finish(self):
        for way in (0, 1):
            for piece in range(len(self.last)):
                for step in range(self.steps(way, piece)):
                    sign = 1 - 2 * way
                    self.copy(way, step, piece, wrap(self.position - sign * step, self.size)).wait_send()


OFFSETS = (0, 1, -1, 2, -2, 3, -3, 4)


def kernel(
    momentum,
    gradient,
    product,
    factor_out,
    xa, xb, part, sibling_part, relay, last_part, gj, gall, pb, up, y_relay, y_last,
    square, ss_z, ss_y, ss_x, ss_c,
    zr_s, zr_r, yr_s, yr_r, sp_s, sp_r, rl_s, rl_r, lp_s, lp_r,
    gz_s, gz_r, gt_s, gt_r, gy_s, gy_r, gs_s, gs_r,
    pr_s, pr_r, ps_s, ps_r, ssy_s, ssy_r, ssx_s, ssx_r, ssc_s, ssc_r,
    ur_s, ur_r, ul_s, ul_r,
):
    row, col = lax.axis_index("row"), lax.axis_index("col")
    z, y = lax.div(row, Y), lax.rem(row, Y)
    x, core = lax.div(col, 2), lax.rem(col, 2)
    other = 1 - core

    def at_z(p):
        return (p * Y + y, col)

    def at_y(p):
        return (z * Y + p, col)

    def at_x(p):
        return (row, p * 2 + core)

    sibling = (row, x * 2 + other)

    barrier = pltpu.get_barrier_semaphore()
    partners = [at_z(wrap(z + 1, Z)), at_z(wrap(z - 1, Z)), sibling]
    partners += [at_y(wrap(y + d, Y)) for d in (1, 2, 3)]
    partners += [at_x(wrap(x + d, X)) for d in (1, 2, 3)]
    for partner in partners:
        pl.semaphore_signal(barrier, inc=1, device_id=partner, device_id_type=pl.DeviceIdType.MESH)
    iterate = (decay_rate * momentum[...] + gradient[...].astype(F32)).astype(BF16)
    xb[z] = iterate
    xa[y] = iterate
    pl.semaphore_wait(barrier, len(partners))

    zr = Ring(Z, z, at_z, lambda b, p: xb.at[b, pl.ds(p * HALF, HALF)], (0, 1), zr_s, zr_r)
    yr = Ring(Y, y, at_y, lambda b, p: xa.at[b, pl.ds(p * HALF, HALF)], (0, 1), yr_s, yr_r)
    for way, piece in ((0, 0), (1, 1), (0, 1), (1, 0)):
        zr.send(way, 0, piece)
        yr.send(way, 0, piece)

    def z_of(event):
        return wrap(z + OFFSETS[event], Z)

    def sibling_copy(there):
        return remote(
            part.at[there, other], sibling_part.at[there], sp_s.at[there], sp_r.at[there], sibling
        )

    def form(event):
        there = z_of(event)
        block = xb[there]
        part[there] = lax.dot_general(
            block, xa[...].reshape(WIDE, COLS), NT, preferred_element_type=F32
        ).reshape(2, HALF, WIDE)
        sibling_copy(there).start()
        wide = block.astype(F32)
        ss_z[there] = jnp.broadcast_to(jnp.sum(wide * wide, keepdims=True), (8, 128))

    def role_of(there):
        return wrap(x - lax.rem(there, X), X)

    def relay_copy(there, side):
        place = pl.ds(side * (HALF // 2), HALF // 2)
        return remote(
            part.at[there, core, place],
            relay.at[there],
            rl_s.at[there, side],
            rl_r.at[there],
            at_x(wrap(x - 1 + 2 * side, X)),
        )

    def last_copy(there, role):
        side = lax.div(role, 2)
        half = lax.div(there, X)
        return remote(
            part.at[there, core],
            last_part.at[half, side],
            lp_s.at[there],
            lp_r.at[half, side],
            at_x(wrap(x + role - 2, X)),
        )

    def join(event):
        there = z_of(event)
        sibling_copy(there).wait_recv()
        part[there, core] = part[there, core] + sibling_part[there]

        @pl.when(role_of(there) == 2)
        def _():
            relay_copy(there, 0).start()
            relay_copy(there, 1).start()

    def pass_on(event):
        there = z_of(event)
        role = role_of(there)

        @pl.when(lax.rem(role, 2) == 1)
        def _():
            relay_copy(there, 0).wait_recv()
            place = pl.ds(pl.multiple_of(lax.div(role, 2) * (HALF // 2), 8), HALF // 2)
            part[there, core, place] = part[there, core, place] + relay[there]
            last_copy(there, role).start()

    cut = ((0, 48), (48, 32))
    gz = Ring(Z, z, at_z, lambda b, p: gj.at[b, p], (0, 1), gz_s, gz_r)
    gy = []
    for event in range(Z):
        there = z_of(event)
        gy.append(
            Ring(
                Y,
                y,
                at_y,
                lambda b, p, there=there: gall.at[there, b, core, pl.ds(*cut[p])],
                (0, 1),
                gy_s.at[there],
                gy_r.at[there],
            )
        )

    def last_wait(half, side):
        there = half * X + x
        remote(
            part.at[there, core], last_part.at[half, side], lp_s.at[there], lp_r.at[half, side], sibling
        ).wait_recv()

    def tile_copy(there, d):
        place = gall.at[there, y, core]
        return remote(place, place, gt_s.at[there, d - 1], gt_r.at[there], at_x(wrap(x + d, X)))

    def settle(event):
        there = z_of(event)
        half = lax.div(there, X)

        @pl.when(role_of(there) == 0)
        def _():
            last_wait(half, 0)
            last_wait(half, 1)
            tile = (part[there, core] + last_part[half, 0] + last_part[half, 1]).astype(BF16)
            gj[z, half] = tile
            gall[there, y, core] = tile
            for d in (1, 3, 2):
                tile_copy(there, d).start()
            gz.send(0, 0, half)
            gz.send(1, 0, half)

    def share(there, k, core_):
        place = gall.at[there, wrap(y + k, Y), core_]
        return remote(place, place, gs_s.at[there, k], gs_r.at[there, k], sibling)

    def spread(event):
        there = z_of(event)

        @pl.when(role_of(there) != 0)
        def _():
            tile_copy(there, 1).wait_recv()

        gy[event].start(0)
        gy[event].start(1)
        share(there, 0, core).start()

    def meet(event):
        for way, piece in ((0, 0), (1, 1), (0, 1), (1, 0)):
            gy[event].recv(way, 0, piece)
        share(z_of(event), 1, core).start()
        share(z_of(event), 3, core).start()

    def close(event):
        gy[event].recv(0, 1, 0)
        gy[event].recv(1, 1, 1)
        share(z_of(event), 2, core).start()

    def multiply(event):
        there = z_of(event)
        for k in (0, 1, 3, 2):
            share(there, k, other).wait_recv()
        square[...] += jnp.dot(
            gj[there].reshape(ROWS, WIDE), gall[there].reshape(WIDE, WIDE), preferred_element_type=F32
        )

    def first(ring, step):
        ring.recv(0, step, 0)
        ring.recv(1, step, 1)

    def second(ring, step):
        ring.recv(0, step, 1)
        ring.recv(1, step, 0)

    def small(refs, slot, send_sems, recv_sems, index, device):
        return remote(refs.at[slot], refs.at[slot], send_sems.at[index], recv_sems.at[index], device)

    square[...] = jnp.zeros_like(square)
    first(zr, 0)
    first(yr, 0)
    second(zr, 0)
    second(yr, 0)
    first(zr, 1)
    first(yr, 1)
    for event in (0, 1, 2):
        form(event)
    for event in (0, 1, 2):
        join(event)
    second(zr, 1)
    form(3)
    form(4)
    join(3)
    join(4)
    for event in (0, 1, 2):
        pass_on(event)
    first(zr, 2)
    pass_on(3)
    pass_on(4)
    second(zr, 2)
    form(5)
    form(6)
    settle(0)
    join(5)
    join(6)
    first(zr, 3)
    form(7)

    total = ss_z[0]
    for k in range(1, Z):
        total = total + ss_z[k]
    ss_y[y] = total
    for d in (1, 2, 3):
        small(ss_y, y, ssy_s, ssy_r, d - 1, at_y(wrap(y + d, Y))).start()

    settle(1)
    settle(2)
    join(7)
    settle(3)
    settle(4)
    pass_on(5)
    pass_on(6)
    spread(0)
    spread(1)
    spread(2)
    pass_on(7)
    spread(3)
    spread(4)

    for d in (1, 2, 3):
        small(ss_y, wrap(y - d, Y), ssy_s, ssy_r, d - 1, sibling).wait_recv()
    ss_x[x] = ss_y[0] + ss_y[1] + ss_y[2] + ss_y[3]
    for d in (1, 2, 3):
        small(ss_x, x, ssx_s, ssx_r, d - 1, at_x(wrap(x + d, X))).start()

    meet(0)
    settle(5)
    settle(6)
    meet(1)
    meet(2)
    settle(7)
    meet(3)
    meet(4)
    spread(5)
    spread(6)
    close(0)
    close(1)
    close(2)
    spread(7)
    close(3)
    close(4)
    first(gz, 0)
    second(gz, 0)

    for d in (1, 2, 3):
        small(ss_x, wrap(x - d, X), ssx_s, ssx_r, d - 1, sibling).wait_recv()
    ss_c[core] = ss_x[0] + ss_x[1] + ss_x[2] + ss_x[3]
    small(ss_c, core, ssc_s, ssc_r, 0, sibling).start()

    meet(5)
    meet(6)
    first(gz, 1)
    second(gz, 1)
    meet(7)
    multiply(0)
    multiply(1)
    multiply(2)
    close(5)
    close(6)
    first(gz, 2)
    second(gz, 2)
    close(7)
    multiply(3)
    multiply(4)
    small(ss_c, other, ssc_s, ssc_r, 0, sibling).wait_recv()
    norm_total = (ss_c[0] + ss_c[1])[0:1, 0:1]
    factor = math.sqrt(FULL_ROWS) / (3.0 * (jnp.sqrt(norm_total) + norm_eps))
    factor_out[...] = jnp.broadcast_to(math.sqrt(FULL_COLS) * factor, factor_out.shape)
    multiply(5)
    multiply(6)
    first(gz, 3)
    multiply(7)

    pr = Ring(X, x, at_x, lambda b, p: pb.at[p, b, core], (0, 1), pr_s, pr_r)
    for half in (0, 1):
        gram = gj[z, half].astype(F32)
        tile = (
            cubic_coef * factor * factor * gram
            + quintic_coef * (factor * factor) * (factor * factor) * square[pl.ds(half * HALF, HALF)]
        )
        pb[half, x, core] = tile.astype(BF16)
        pr.start(half)

    def share_p(index, core_):
        place = pb.at[:, wrap(x + index, X), core_]
        return remote(place, place, ps_s.at[index], ps_r.at[index], sibling)

    share_p(0, core).start()
    first(pr, 0)
    second(pr, 0)
    share_p(1, core).start()
    share_p(3, core).start()
    first(pr, 1)
    share_p(2, core).start()
    for index in (0, 1, 3, 2):
        share_p(index, other).wait_recv()

    def y_relay_copy(tile, side):
        return remote(
            up.at[tile, wrap(y + 2, Y), pl.ds(side * HALF, HALF)],
            y_relay.at[tile, side],
            ur_s.at[tile, side],
            ur_r.at[tile, side],
            at_y(wrap(y + 1 - 2 * side, Y)),
        )

    def y_last_copy(tile, side, half):
        return remote(
            up.at[tile, wrap(y + 1 - 2 * side, Y), pl.ds(half * HALF, HALF)],
            y_last.at[tile, side, pl.ds(half * HALF, HALF)],
            ul_s.at[tile, side, half],
            ul_r.at[tile, side, half],
            at_y(wrap(y + 1 - 2 * side, Y)),
        )

    def add_relay(tile):
        for side in (0, 1):
            y_relay_copy(tile, side).wait_recv()
            near = wrap(y + 1 - 2 * side, Y)
            place = pl.ds(side * HALF, HALF)
            up[tile, near, place] = up[tile, near, place] + y_relay[tile, side]
            y_last_copy(tile, side, side).start()

    for tile in range(TILES):
        up[tile] = lax.dot_general(
            pb[...].reshape(Z * ROWS, WIDE),
            xb[:, :, pl.ds(tile * TILE, TILE)].reshape(Z * ROWS, TILE),
            TN,
            preferred_element_type=F32,
        ).reshape(Y, ROWS, TILE)
        for side in (0, 1):
            y_relay_copy(tile, side).start()
        for side in (0, 1):
            y_last_copy(tile, side, 1 - side).start()
    for tile in range(TILES):
        add_relay(tile)
    for tile in range(TILES):
        for side in (0, 1):
            for half in (0, 1):
                y_last_copy(tile, side, half).wait_recv()
        columns = pl.ds(tile * TILE, TILE)
        product[:, columns] = (
            linear_coef * xb[z, :, columns].astype(F32) + up[tile, y] + y_last[tile, 0] + y_last[tile, 1]
        )

    for ring in (zr, yr, gz, pr, *gy):
        ring.finish()
    for event in range(Z):
        there = z_of(event)
        sibling_copy(there).wait_send()
        role = role_of(there)

        @pl.when(role == 2)
        def _():
            relay_copy(there, 0).wait_send()
            relay_copy(there, 1).wait_send()

        @pl.when(lax.rem(role, 2) == 1)
        def _():
            last_copy(there, role).wait_send()

        @pl.when(role == 0)
        def _():
            for d in (1, 2, 3):
                tile_copy(there, d).wait_send()

        for k in range(Y):
            share(there, k, core).wait_send()

    for d in (1, 2, 3):
        small(ss_y, y, ssy_s, ssy_r, d - 1, sibling).wait_send()
        small(ss_x, x, ssx_s, ssx_r, d - 1, sibling).wait_send()
    small(ss_c, core, ssc_s, ssc_r, 0, sibling).wait_send()
    for index in range(4):
        share_p(index, core).wait_send()
    for tile in range(TILES):
        for side in (0, 1):
            y_relay_copy(tile, side).wait_send()
            for half in (0, 1):
                y_last_copy(tile, side, half).wait_send()


def dma(*shape):
    return pltpu.SemaphoreType.DMA(shape)


def twice(*shape):
    return [dma(*shape), dma(*shape)]


def fused(momentum, gradient):
    vmem = pl.BlockSpec(memory_space=pltpu.VMEM)
    return pl.pallas_call(
        kernel,
        out_shape=(
            jax.ShapeDtypeStruct((ROWS, COLS), F32),
            jax.ShapeDtypeStruct((1, COLS), F32),
        ),
        in_specs=[vmem, vmem],
        out_specs=(vmem, vmem),
        scratch_shapes=[
            pltpu.VMEM((Y, ROWS, COLS), BF16),
            pltpu.VMEM((Z, ROWS, COLS), BF16),
            pltpu.VMEM((Z, 2, HALF, WIDE), F32),
            pltpu.VMEM((Z, HALF, WIDE), F32),
            pltpu.VMEM((Z, HALF // 2, WIDE), F32),
            pltpu.VMEM((2, 2, HALF, WIDE), F32),
            pltpu.VMEM((Z, 2, HALF, WIDE), BF16),
            pltpu.VMEM((Z, Y, 2, HALF, WIDE), BF16),
            pltpu.VMEM((2, X, 2, HALF, WIDE), BF16),
            pltpu.VMEM((TILES, Y, ROWS, TILE), F32),
            pltpu.VMEM((TILES, 2, HALF, TILE), F32),
            pltpu.VMEM((TILES, 2, ROWS, TILE), F32),
            pltpu.VMEM((ROWS, WIDE), F32),
            pltpu.VMEM((Z, 8, 128), F32),
            pltpu.VMEM((Y, 8, 128), F32),
            pltpu.VMEM((X, 8, 128), F32),
            pltpu.VMEM((2, 8, 128), F32),
            *twice(2, 4, 2),
            *twice(2, 2, 2),
            *twice(Z),
            dma(Z, 2), dma(Z),
            dma(Z), dma(2, 2),
            *twice(2, 4, 2),
            dma(Z, 3), dma(Z),
            *twice(Z, 2, 2, 2),
            *twice(Z, Y),
            *twice(2, 2, 2),
            *twice(4),
            *twice(3),
            *twice(3),
            *twice(1),
            *twice(TILES, 2),
            *twice(TILES, 2, 2),
        ],
        compiler_params=pltpu.CompilerParams(
            collective_id=0, has_side_effects=True, vmem_limit_bytes=56 * 1024 * 1024
        ),
    )(momentum, gradient)


def local(momentum, gradient):
    new_momentum = decay_rate * momentum + gradient.astype(F32)
    product, scale = fused(momentum, gradient)
    update = scale * product
    return (new_momentum, update)


def solution(mesh):
    placed = (P("row", "col"), P("row", "col"))
    return jax.shard_map(
        local,
        mesh=mesh,
        in_specs=placed,
        out_specs=(P("row", "col"), P("row", "col")),
        check_vma=False,
    )
```

```python
import math

import jax
import jax.numpy as jnp
from jax import lax
from jax.experimental import pallas as pl
from jax.experimental.pallas import tpu as pltpu
from jax.sharding import PartitionSpec as P

decay_rate = 0.95
linear_coef = 3.4445
cubic_coef = -4.775
quintic_coef = 2.0315
norm_eps = 1e-07

X, Y, Z = 4, 4, 8
ROWS, COLS = 160, 1152
HALF = ROWS // 2
WIDE = Y * ROWS
UNIT = 16
EXTRA = pl.ds(UNIT, UNIT)
TILES = 2
TILE = COLS // 3
SPLIT = TILES * TILE
FULL_ROWS = ROWS * Y * Z
FULL_COLS = COLS * X * 2
NT = (((1,), (1,)), ((), ()))
TN = (((0,), (0,)), ((), ()))
F32 = jnp.float32
BF16 = jnp.bfloat16


def wrap(value, size):
    return lax.rem(value + size, size)


def remote(src, dst, send_sem, recv_sem, device):
    return pltpu.make_async_remote_copy(
        src_ref=src,
        dst_ref=dst,
        send_sem=send_sem,
        recv_sem=recv_sem,
        device_id=device,
        device_id_type=pl.DeviceIdType.MESH,
    )


class Ring:
    def __init__(self, size, position, device, region, last, send_sems, recv_sems):
        self.size, self.position, self.device = size, position, device
        self.region, self.last = region, last
        self.send_sems, self.recv_sems = send_sems, recv_sems

    def steps(self, way, piece):
        return self.size // 2 - (0 if self.last[piece] == way else 1)

    def copy(self, way, step, piece, block):
        sign = 1 - 2 * way
        place = self.region(block, piece)
        return remote(
            place,
            place,
            self.send_sems.at[way, step, piece],
            self.recv_sems.at[way, step, piece],
            self.device(wrap(self.position + sign, self.size)),
        )

    def send(self, way, step, piece):
        sign = 1 - 2 * way
        self.copy(way, step, piece, wrap(self.position - sign * step, self.size)).start()

    def start(self):
        for way, piece in ((0, 0), (1, 1), (0, 1), (1, 0)):
            self.send(way, 0, piece)

    def recv(self, way, step, piece):
        if step >= self.steps(way, piece):
            return
        sign = 1 - 2 * way
        self.copy(way, step, piece, wrap(self.position - sign * (step + 1), self.size)).wait_recv()
        if step + 1 < self.steps(way, piece):
            self.send(way, step + 1, piece)

    def finish(self):
        for way in (0, 1):
            for piece in range(len(self.last)):
                for step in range(self.steps(way, piece)):
                    sign = 1 - 2 * way
                    self.copy(way, step, piece, wrap(self.position - sign * step, self.size)).wait_send()


OFFSETS = (0, 1, -1, 2, -2, 3, -3, 4)


def kernel(
    momentum,
    gradient,
    product,
    factor_out,
    xa, xb, part, sibling_part, units, extras, gj, gall, pb, up, y_relay, y_last, uz, z_sum,
    square, ss_z, ss_y, ss_x, ss_c,
    zr_s, zr_r, yr_s, yr_r, sp_s, sp_r, us_s, us_r, es_s, es_r,
    gz_s, gz_r, gt_s, gt_r, ge_s, ge_r, gy_s, gy_r, gs_s, gs_r,
    pr_s, pr_r, ps_s, ps_r, ssy_s, ssy_r, ssx_s, ssx_r, ssc_s, ssc_r,
    ur_s, ur_r, ul_s, ul_r, zs_s, zs_r,
):
    row, col = lax.axis_index("row"), lax.axis_index("col")
    z, y = lax.div(row, Y), lax.rem(row, Y)
    x, core = lax.div(col, 2), lax.rem(col, 2)
    other = 1 - core

    def at_z(p):
        return (p * Y + y, col)

    def at_y(p):
        return (z * Y + p, col)

    def at_x(p):
        return (row, p * 2 + core)

    sibling = (row, x * 2 + other)

    barrier = pltpu.get_barrier_semaphore()
    partners = [at_z(wrap(z + 1, Z)), at_z(wrap(z - 1, Z)), sibling]
    partners += [at_y(wrap(y + d, Y)) for d in (1, 2, 3)]
    partners += [at_x(wrap(x + d, X)) for d in (1, 2, 3)]
    for partner in partners:
        pl.semaphore_signal(barrier, inc=1, device_id=partner, device_id_type=pl.DeviceIdType.MESH)
    iterate = (decay_rate * momentum[...] + gradient[...].astype(F32)).astype(BF16)
    xb[z] = iterate
    xa[y] = iterate
    pl.semaphore_wait(barrier, len(partners))

    zr = Ring(Z, z, at_z, lambda b, p: xb.at[b, pl.ds(p * HALF, HALF)], (0, 1), zr_s, zr_r)
    yr = Ring(Y, y, at_y, lambda b, p: xa.at[b, pl.ds(p * HALF, HALF)], (0, 1), yr_s, yr_r)
    for way, piece in ((0, 0), (1, 1), (0, 1), (1, 0)):
        zr.send(way, 0, piece)
        yr.send(way, 0, piece)

    def z_of(event):
        return wrap(z + OFFSETS[event], Z)

    def sibling_copy(there):
        return remote(
            part.at[there, other], sibling_part.at[there], sp_s.at[there], sp_r.at[there], sibling
        )

    def form(event):
        there = z_of(event)
        block = xb[there]
        part[there] = lax.dot_general(
            block, xa[...].reshape(WIDE, COLS), NT, preferred_element_type=F32
        ).reshape(2, HALF, WIDE)
        sibling_copy(there).start()
        wide = block.astype(F32)
        ss_z[there] = jnp.broadcast_to(jnp.sum(wide * wide, keepdims=True), (8, 128))

    def role_of(there):
        return wrap(x - lax.rem(there, X), X)

    def rows_of(unit):
        return pl.ds(pl.multiple_of(UNIT * (unit + lax.div(unit + 2, 3)), UNIT), UNIT)

    def unit_copy(there, d):
        to = wrap(x + d, X)
        return remote(
            part.at[there, core, rows_of(wrap(to - lax.rem(there, X), X))],
            units.at[there, d - 1],
            us_s.at[there, d - 1],
            us_r.at[there, d - 1],
            at_x(to),
        )

    def extra_copy(there, slot):
        return remote(
            part.at[there, core, EXTRA],
            extras.at[there, slot],
            es_s.at[there],
            es_r.at[there, slot],
            at_x(lax.rem(there, X)),
        )

    def join(event):
        there = z_of(event)
        sibling_copy(there).wait_recv()
        part[there, core] = part[there, core] + sibling_part[there]
        for d in (2, 1, 3):
            unit_copy(there, d).start()
        role = role_of(there)

        @pl.when(role != 0)
        def _():
            extra_copy(there, 3 - role).start()

    cut = ((0, 48), (48, 32))
    gz = Ring(Z, z, at_z, lambda b, p: gj.at[b, p], (0, 1), gz_s, gz_r)
    gy = []
    for event in range(Z):
        there = z_of(event)
        gy.append(
            Ring(
                Y,
                y,
                at_y,
                lambda b, p, there=there: gall.at[there, b, core, pl.ds(*cut[p])],
                (0, 1),
                gy_s.at[there],
                gy_r.at[there],
            )
        )

    def tile_copy(there, d):
        place = gall.at[there, y, core, rows_of(role_of(there))]
        return remote(
            place, place, gt_s.at[there, d - 1], gt_r.at[there, d - 1], at_x(wrap(x + d, X))
        )

    def extra_tile_copy(there, d):
        place = gall.at[there, y, core, EXTRA]
        return remote(place, place, ge_s.at[there, d - 1], ge_r.at[there], at_x(wrap(x + d, X)))

    def settle(event):
        there = z_of(event)
        role = role_of(there)
        rows = rows_of(role)
        for d in (1, 2, 3):
            unit_copy(there, d).wait_recv()
        gall[there, y, core, rows] = (
            part[there, core, rows] + units[there, 0] + units[there, 1] + units[there, 2]
        ).astype(BF16)
        for d in (2, 1, 3):
            tile_copy(there, d).start()

        @pl.when(role == 0)
        def _():
            for slot in (0, 1, 2):
                extra_copy(there, slot).wait_recv()
            gall[there, y, core, EXTRA] = (
                part[there, core, EXTRA] + extras[there, 0] + extras[there, 1] + extras[there, 2]
            ).astype(BF16)
            for d in (2, 1, 3):
                extra_tile_copy(there, d).start()

    def share(there, k, core_):
        place = gall.at[there, wrap(y + k, Y), core_]
        return remote(place, place, gs_s.at[there, k], gs_r.at[there, k], sibling)

    def spread(event):
        there = z_of(event)
        role = role_of(there)
        for d in (1, 2, 3):
            place = gall.at[there, y, core, rows_of(wrap(role - d, X))]
            remote(place, place, gt_s.at[there, d - 1], gt_r.at[there, d - 1], sibling).wait_recv()

        @pl.when(role != 0)
        def _():
            extra_tile_copy(there, 1).wait_recv()

        gy[event].start()
        share(there, 0, core).start()

        @pl.when(role == 0)
        def _():
            half = lax.div(there, X)
            gj[z, half] = gall[there, y, core]
            gz.send(0, 0, half)
            gz.send(1, 0, half)

    def meet(event):
        for way, piece in ((0, 0), (1, 1), (0, 1), (1, 0)):
            gy[event].recv(way, 0, piece)
        share(z_of(event), 1, core).start()
        share(z_of(event), 3, core).start()

    def close(event):
        gy[event].recv(0, 1, 0)
        gy[event].recv(1, 1, 1)
        share(z_of(event), 2, core).start()

    def multiply(event):
        there = z_of(event)
        for k in (0, 1, 3, 2):
            share(there, k, other).wait_recv()
        square[...] += jnp.dot(
            gj[there].reshape(ROWS, WIDE), gall[there].reshape(WIDE, WIDE), preferred_element_type=F32
        )

    def first(ring, step):
        ring.recv(0, step, 0)
        ring.recv(1, step, 1)

    def second(ring, step):
        ring.recv(0, step, 1)
        ring.recv(1, step, 0)

    def small(refs, slot, send_sems, recv_sems, index, device):
        return remote(refs.at[slot], refs.at[slot], send_sems.at[index], recv_sems.at[index], device)

    square[...] = jnp.zeros_like(square)
    first(zr, 0)
    first(yr, 0)
    second(zr, 0)
    second(yr, 0)
    first(zr, 1)
    first(yr, 1)
    for event in (0, 1, 2):
        form(event)
    for event in (0, 1, 2):
        join(event)
    second(zr, 1)
    form(3)
    form(4)
    settle(0)
    first(zr, 2)
    settle(1)
    settle(2)
    join(3)
    join(4)
    second(zr, 2)
    form(5)
    form(6)
    spread(0)
    join(5)
    join(6)
    spread(1)
    spread(2)
    first(zr, 3)
    form(7)
    settle(3)
    settle(4)
    join(7)

    total = ss_z[0]
    for k in range(1, Z):
        total = total + ss_z[k]
    ss_y[y] = total
    for d in (1, 2, 3):
        small(ss_y, y, ssy_s, ssy_r, d - 1, at_y(wrap(y + d, Y))).start()

    meet(0)
    spread(3)
    meet(1)
    spread(4)
    settle(5)
    settle(6)
    meet(2)
    close(0)

    for d in (1, 2, 3):
        small(ss_y, wrap(y - d, Y), ssy_s, ssy_r, d - 1, sibling).wait_recv()
    ss_x[x] = ss_y[0] + ss_y[1] + ss_y[2] + ss_y[3]
    for d in (1, 2, 3):
        small(ss_x, x, ssx_s, ssx_r, d - 1, at_x(wrap(x + d, X))).start()

    settle(7)
    close(1)
    spread(5)
    spread(6)
    meet(3)
    close(2)
    meet(4)
    spread(7)
    first(gz, 0)
    second(gz, 0)
    close(3)
    close(4)

    for d in (1, 2, 3):
        small(ss_x, wrap(x - d, X), ssx_s, ssx_r, d - 1, sibling).wait_recv()
    ss_c[core] = ss_x[0] + ss_x[1] + ss_x[2] + ss_x[3]
    small(ss_c, core, ssc_s, ssc_r, 0, sibling).start()

    meet(5)
    meet(6)
    first(gz, 1)
    second(gz, 1)
    meet(7)
    multiply(0)
    multiply(1)
    multiply(2)
    close(5)
    close(6)
    first(gz, 2)
    second(gz, 2)
    close(7)
    multiply(3)
    multiply(4)
    small(ss_c, other, ssc_s, ssc_r, 0, sibling).wait_recv()
    norm_total = (ss_c[0] + ss_c[1])[0:1, 0:1]
    factor = math.sqrt(FULL_ROWS) / (3.0 * (jnp.sqrt(norm_total) + norm_eps))
    factor_out[...] = jnp.broadcast_to(math.sqrt(FULL_COLS) * factor, factor_out.shape)
    multiply(5)
    multiply(6)
    first(gz, 3)
    multiply(7)

    pr = Ring(X, x, at_x, lambda b, p: pb.at[p, b, core], (0, 1), pr_s, pr_r)
    for half in (0, 1):
        gram = gj[z, half].astype(F32)
        tile = (
            cubic_coef * factor * factor * gram
            + quintic_coef * (factor * factor) * (factor * factor) * square[pl.ds(half * HALF, HALF)]
        )
        pb[half, x, core] = tile.astype(BF16)
    pr.start()

    def share_p(index, core_):
        place = pb.at[:, wrap(x + index, X), core_]
        return remote(place, place, ps_s.at[index], ps_r.at[index], sibling)

    share_p(0, core).start()
    first(pr, 0)
    second(pr, 0)
    share_p(1, core).start()
    share_p(3, core).start()
    first(pr, 1)
    share_p(2, core).start()
    for index in (0, 1, 3, 2):
        share_p(index, other).wait_recv()

    def y_relay_copy(tile, side):
        return remote(
            up.at[tile, wrap(y + 2, Y), pl.ds(side * HALF, HALF)],
            y_relay.at[tile, side],
            ur_s.at[tile, side],
            ur_r.at[tile, side],
            at_y(wrap(y + 1 - 2 * side, Y)),
        )

    def y_last_copy(tile, side, half):
        return remote(
            up.at[tile, wrap(y + 1 - 2 * side, Y), pl.ds(half * HALF, HALF)],
            y_last.at[tile, side, pl.ds(half * HALF, HALF)],
            ul_s.at[tile, side, half],
            ul_r.at[tile, side, half],
            at_y(wrap(y + 1 - 2 * side, Y)),
        )

    def add_relay(tile):
        for side in (0, 1):
            y_relay_copy(tile, side).wait_recv()
            near = wrap(y + 1 - 2 * side, Y)
            place = pl.ds(side * HALF, HALF)
            up[tile, near, place] = up[tile, near, place] + y_relay[tile, side]
            y_last_copy(tile, side, side).start()

    def z_sum_copy(way, step, half):
        sign = 1 - 2 * way
        return remote(
            uz.at[wrap(z + sign * (4 - step), Z), pl.ds(half * HALF, HALF)],
            z_sum.at[way, step, half],
            zs_s.at[way, step, half],
            zs_r.at[way, step, half],
            at_z(wrap(z + sign, Z)),
        )

    def z_sum_step(step, second_half):
        for way in (0, 1):
            half = way if not second_half else 1 - way
            z_sum_copy(way, step, half).wait_recv()
            near = wrap(z + (1 - 2 * way) * (3 - step), Z)
            place = pl.ds(half * HALF, HALF)
            uz[near, place] = uz[near, place] + z_sum[way, step, half]
            z_sum_copy(way, step + 1, half).start()

    def begin_z():
        uz[...] = jnp.dot(
            pb[...].reshape(Z * ROWS, WIDE),
            xa[:, :, pl.ds(SPLIT, TILE)].reshape(WIDE, TILE),
            preferred_element_type=F32,
        ).reshape(Z, ROWS, TILE)
        for way in (0, 1):
            z_sum_copy(way, 0, way).start()
        for way in (0, 1):
            z_sum_copy(way, 1, 1 - way).start()

    def begin_y(tile):
        up[tile] = lax.dot_general(
            pb[...].reshape(Z * ROWS, WIDE),
            xb[:, :, pl.ds(tile * TILE, TILE)].reshape(Z * ROWS, TILE),
            TN,
            preferred_element_type=F32,
        ).reshape(Y, ROWS, TILE)
        for side in (0, 1):
            y_relay_copy(tile, side).start()

    def begin_near(tile):
        for side in (0, 1):
            y_last_copy(tile, side, 1 - side).start()

    def finish_y(tile):
        for side in (0, 1):
            for half in (0, 1):
                y_last_copy(tile, side, half).wait_recv()
        columns = pl.ds(tile * TILE, TILE)
        product[:, columns] = (
            linear_coef * xb[z, :, columns].astype(F32) + up[tile, y] + y_last[tile, 0] + y_last[tile, 1]
        )

    def finish_z(half):
        for way in (0, 1):
            z_sum_copy(way, 3, half).wait_recv()
        rows, columns = pl.ds(half * HALF, HALF), pl.ds(SPLIT, TILE)
        product[rows, columns] = (
            linear_coef * xb[z, rows, columns].astype(F32)
            + uz[z, rows]
            + z_sum[0, 3, half]
            + z_sum[1, 3, half]
        )

    begin_z()
    begin_y(0)
    begin_y(1)
    begin_near(0)
    begin_near(1)
    z_sum_step(0, False)
    add_relay(0)
    z_sum_step(1, True)
    add_relay(1)
    z_sum_step(1, False)
    z_sum_step(2, True)
    z_sum_step(2, False)
    finish_y(0)
    finish_y(1)
    finish_z(0)
    finish_z(1)

    for ring in (zr, yr, gz, pr, *gy):
        ring.finish()
    for event in range(Z):
        there = z_of(event)
        sibling_copy(there).wait_send()
        role = role_of(there)
        for d in (1, 2, 3):
            unit_copy(there, d).wait_send()
            tile_copy(there, d).wait_send()

        @pl.when(role != 0)
        def _():
            extra_copy(there, 3 - role).wait_send()

        @pl.when(role == 0)
        def _():
            for d in (1, 2, 3):
                extra_tile_copy(there, d).wait_send()

        for k in range(Y):
            share(there, k, core).wait_send()

    for d in (1, 2, 3):
        small(ss_y, y, ssy_s, ssy_r, d - 1, sibling).wait_send()
        small(ss_x, x, ssx_s, ssx_r, d - 1, sibling).wait_send()
    small(ss_c, core, ssc_s, ssc_r, 0, sibling).wait_send()
    for index in range(4):
        share_p(index, core).wait_send()
    for tile in range(TILES):
        for side in (0, 1):
            y_relay_copy(tile, side).wait_send()
            for half in (0, 1):
                y_last_copy(tile, side, half).wait_send()
    for way in (0, 1):
        z_sum_copy(way, 0, way).wait_send()
        for step in (1, 2, 3):
            for half in (0, 1):
                z_sum_copy(way, step, half).wait_send()


def dma(*shape):
    return pltpu.SemaphoreType.DMA(shape)


def twice(*shape):
    return [dma(*shape), dma(*shape)]


def fused(momentum, gradient):
    vmem = pl.BlockSpec(memory_space=pltpu.VMEM)
    return pl.pallas_call(
        kernel,
        out_shape=(
            jax.ShapeDtypeStruct((ROWS, COLS), F32),
            jax.ShapeDtypeStruct((8, COLS), F32),
        ),
        in_specs=[vmem, vmem],
        out_specs=(vmem, vmem),
        scratch_shapes=[
            pltpu.VMEM((Y, ROWS, COLS), BF16),
            pltpu.VMEM((Z, ROWS, COLS), BF16),
            pltpu.VMEM((Z, 2, HALF, WIDE), F32),
            pltpu.VMEM((Z, HALF, WIDE), F32),
            pltpu.VMEM((Z, 3, UNIT, WIDE), F32),
            pltpu.VMEM((Z, 3, UNIT, WIDE), F32),
            pltpu.VMEM((Z, 2, HALF, WIDE), BF16),
            pltpu.VMEM((Z, Y, 2, HALF, WIDE), BF16),
            pltpu.VMEM((2, X, 2, HALF, WIDE), BF16),
            pltpu.VMEM((TILES, Y, ROWS, TILE), F32),
            pltpu.VMEM((TILES, 2, HALF, TILE), F32),
            pltpu.VMEM((TILES, 2, ROWS, TILE), F32),
            pltpu.VMEM((Z, ROWS, TILE), F32),
            pltpu.VMEM((2, 4, 2, HALF, TILE), F32),
            pltpu.VMEM((ROWS, WIDE), F32),
            pltpu.VMEM((Z, 8, 128), F32),
            pltpu.VMEM((Y, 8, 128), F32),
            pltpu.VMEM((X, 8, 128), F32),
            pltpu.VMEM((2, 8, 128), F32),
            *twice(2, 4, 2),
            *twice(2, 2, 2),
            *twice(Z),
            *twice(Z, 3),
            dma(Z), dma(Z, 3),
            *twice(2, 4, 2),
            *twice(Z, 3),
            dma(Z, 3), dma(Z),
            *twice(Z, 2, 2, 2),
            *twice(Z, Y),
            *twice(2, 2, 2),
            *twice(4),
            *twice(3),
            *twice(3),
            *twice(1),
            *twice(TILES, 2),
            *twice(TILES, 2, 2),
            *twice(2, 4, 2),
        ],
        compiler_params=pltpu.CompilerParams(
            collective_id=0, has_side_effects=True, vmem_limit_bytes=56 * 1024 * 1024
        ),
    )(momentum, gradient)


def local(momentum, gradient):
    new_momentum = decay_rate * momentum + gradient.astype(F32)
    product, scale = fused(momentum, gradient)
    update = (scale * product.reshape(ROWS // 8, 8, COLS)).reshape(ROWS, COLS)
    return (new_momentum, update)


def solution(mesh):
    placed = (P("row", "col"), P("row", "col"))
    return jax.shard_map(
        local,
        mesh=mesh,
        in_specs=placed,
        out_specs=(P("row", "col"), P("row", "col")),
        check_vma=False,
    )
```

```python
import math

import jax
import jax.numpy as jnp
from jax import lax
from jax.experimental import pallas as pl
from jax.experimental.pallas import tpu as pltpu
from jax.sharding import PartitionSpec as P

decay_rate = 0.95
linear_coef = 3.4445
cubic_coef = -4.775
quintic_coef = 2.0315
norm_eps = 1e-07

X, Y, Z = 4, 4, 8
ROWS, COLS = 160, 1152
HALF = ROWS // 2
WIDE = Y * ROWS
UNIT = 16
EXTRA = pl.ds(UNIT, UNIT)
TILES = 2
TILE = COLS // 3
SPLIT = TILES * TILE
FULL_ROWS = ROWS * Y * Z
FULL_COLS = COLS * X * 2
NT = (((1,), (1,)), ((), ()))
TN = (((0,), (0,)), ((), ()))
F32 = jnp.float32
BF16 = jnp.bfloat16


def wrap(value, size):
    return lax.rem(value + size, size)


def remote(src, dst, send_sem, recv_sem, device):
    return pltpu.make_async_remote_copy(
        src_ref=src,
        dst_ref=dst,
        send_sem=send_sem,
        recv_sem=recv_sem,
        device_id=device,
        device_id_type=pl.DeviceIdType.MESH,
    )


class Ring:
    def __init__(self, size, position, device, region, last, send_sem, recv_sems):
        self.size, self.position, self.device = size, position, device
        self.region, self.last = region, last
        self.send_sem, self.recv_sems = send_sem, recv_sems
        self.slots = {}
        for way in (0, 1):
            for piece in range(len(last)):
                for step in range(size // 2 - (0 if last[piece] == way else 1)):
                    self.slots[way, step, piece] = len(self.slots)

    def copy(self, way, step, piece, block):
        sign = 1 - 2 * way
        place = self.region(block, piece)
        return remote(
            place,
            place,
            self.send_sem,
            self.recv_sems.at[self.slots[way, step, piece]],
            self.device(wrap(self.position + sign, self.size)),
        )

    def send(self, way, step, piece):
        sign = 1 - 2 * way
        self.copy(way, step, piece, wrap(self.position - sign * step, self.size)).start()

    def start(self):
        for way, piece in ((0, 0), (1, 1), (0, 1), (1, 0)):
            self.send(way, 0, piece)

    def recv(self, way, step, piece):
        if (way, step, piece) not in self.slots:
            return
        sign = 1 - 2 * way
        self.copy(way, step, piece, wrap(self.position - sign * (step + 1), self.size)).wait_recv()
        if (way, step + 1, piece) in self.slots:
            self.send(way, step + 1, piece)


OFFSETS = (0, 1, -1, 2, -2, 3, -3, 4)


def kernel(
    momentum,
    gradient,
    product,
    factor_out,
    xa, xb, part, sibling_part, units, gj, gall, pb, up, y_relay, y_last, uz, z_sum,
    square, ss_z, ss_y, ss_x, ss_c,
    sent, zr_r, yr_r, sp_r, us_r, gz_r, gt_r, gy_r, gs_r, pr_r, ps_r, ss_r, ur_r, ul_r, zs_r,
):
    row, col = lax.axis_index("row"), lax.axis_index("col")
    z, y = lax.div(row, Y), lax.rem(row, Y)
    x, core = lax.div(col, 2), lax.rem(col, 2)
    other = 1 - core

    def at_z(p):
        return (p * Y + y, col)

    def at_y(p):
        return (z * Y + p, col)

    def at_x(p):
        return (row, p * 2 + core)

    sibling = (row, x * 2 + other)

    barrier = pltpu.get_barrier_semaphore()
    partners = [at_z(wrap(z + d, Z)) for d in (1, -1, 2, -2)] + [sibling]
    partners += [at_y(wrap(y + d, Y)) for d in (1, 2, 3)]
    partners += [at_x(wrap(x + d, X)) for d in (1, 2, 3)]
    for partner in partners:
        pl.semaphore_signal(barrier, inc=1, device_id=partner, device_id_type=pl.DeviceIdType.MESH)
    iterate = (decay_rate * momentum[...] + gradient[...].astype(F32)).astype(BF16)
    xb[z] = iterate
    xa[y] = iterate
    pl.semaphore_wait(barrier, len(partners))

    zr = Ring(Z, z, at_z, lambda b, p: xb.at[b, pl.ds(p * HALF, HALF)], (0, 1), sent.at[0], zr_r)
    yr = Ring(Y, y, at_y, lambda b, p: xa.at[b, pl.ds(p * HALF, HALF)], (0, 1), sent.at[1], yr_r)
    for way, piece in ((0, 0), (1, 1), (0, 1), (1, 0)):
        zr.send(way, 0, piece)
        yr.send(way, 0, piece)

    def z_of(event):
        return wrap(z + OFFSETS[event], Z)

    def sibling_copy(there):
        return remote(
            part.at[there, other], sibling_part.at[there], sent.at[2], sp_r.at[there], sibling
        )

    def form(event):
        there = z_of(event)
        block = xb[there]
        part[there] = lax.dot_general(
            block, xa[...].reshape(WIDE, COLS), NT, preferred_element_type=F32
        ).reshape(2, HALF, WIDE)
        sibling_copy(there).start()
        wide = block.astype(F32)
        ss_z[there] = jnp.broadcast_to(jnp.sum(wide * wide, keepdims=True), (8, 128))

    def role_of(there):
        return wrap(x - lax.rem(there, X), X)

    def rows_of(unit):
        return pl.ds(pl.multiple_of(UNIT * (unit + lax.div(unit + 2, 3)), UNIT), UNIT)

    def unit_copy(there, d):
        to = wrap(x + d, X)
        return remote(
            part.at[there, core, rows_of(wrap(to - lax.rem(there, X), X))],
            units.at[there, d - 1],
            sent.at[3],
            us_r.at[there],
            at_x(to),
        )

    def extra_copy(there, slot):
        return remote(
            part.at[there, core, EXTRA],
            units.at[there, 3 + slot],
            sent.at[3],
            us_r.at[there],
            at_x(lax.rem(there, X)),
        )

    def join(event):
        there = z_of(event)
        sibling_copy(there).wait_recv()
        part[there, core] = part[there, core] + sibling_part[there]
        for d in (2, 1, 3):
            unit_copy(there, d).start()
        role = role_of(there)

        @pl.when(role != 0)
        def _():
            extra_copy(there, 3 - role).start()

    cut = ((0, 48), (48, 32))
    def panel_copy(way, hops, block, slot, piece):
        place = gj.at[block, piece]
        return remote(
            place, place, sent.at[4], gz_r.at[slot], at_z(wrap(z + (1 - 2 * way) * hops, Z))
        )

    def panel_start(piece):
        for hops in (2, 1):
            for way in (0, 1):
                panel_copy(way, hops, z, 4 * (hops - 1) + 2 * way + piece, piece).start()

    def panel_wait(distance):
        for way in (0, 1):
            for piece in (0, 1) if distance < 4 else (way,):
                slot = 4 * (distance - 1) + (2 * way + piece if distance < 4 else way)
                block = wrap(z - (1 - 2 * way) * distance, Z)
                panel_copy(way, 1, block, slot, piece).wait_recv()
                if distance == 2:
                    if piece == way:
                        panel_copy(way, 2, block, 12 + way, piece).start()
                    panel_copy(way, 1, block, 8 + 2 * way + piece, piece).start()

    gy = []
    for event in range(Z):
        there = z_of(event)
        gy.append(
            Ring(
                Y,
                y,
                at_y,
                lambda b, p, there=there: gall.at[there, b, core, pl.ds(*cut[p])],
                (0, 1),
                sent.at[6],
                gy_r.at[there],
            )
        )

    def tile_copy(there, d):
        place = gall.at[there, y, core, rows_of(role_of(there))]
        return remote(place, place, sent.at[5], gt_r.at[there], at_x(wrap(x + d, X)))

    def extra_tile_copy(there, d):
        place = gall.at[there, y, core, EXTRA]
        return remote(place, place, sent.at[5], gt_r.at[there], at_x(wrap(x + d, X)))

    def landed(place, sem):
        remote(place, place, sent.at[0], sem, sibling).wait_recv()

    def settle(event):
        there = z_of(event)
        role = role_of(there)
        rows = rows_of(role)

        @pl.when(role == 0)
        def _():
            landed(units.at[there], us_r.at[there])
            gall[there, y, core, EXTRA] = (
                part[there, core, EXTRA] + units[there, 3] + units[there, 4] + units[there, 5]
            ).astype(BF16)
            for d in (2, 1, 3):
                extra_tile_copy(there, d).start()

        @pl.when(role != 0)
        def _():
            landed(units.at[there, pl.ds(0, 3)], us_r.at[there])

        gall[there, y, core, rows] = (
            part[there, core, rows] + units[there, 0] + units[there, 1] + units[there, 2]
        ).astype(BF16)
        for d in (2, 1, 3):
            tile_copy(there, d).start()

    def share(there, k, core_):
        place = gall.at[there, wrap(y + k, Y), core_]
        return remote(place, place, sent.at[7], gs_r.at[there], sibling)

    def spread(event):
        there = z_of(event)
        role = role_of(there)
        @pl.when(role == 0)
        def _():
            landed(gall.at[there, y, core, pl.ds(0, 3 * UNIT)], gt_r.at[there])

        @pl.when(role != 0)
        def _():
            landed(gall.at[there, y, core, pl.ds(0, 4 * UNIT)], gt_r.at[there])

        gy[event].start()
        share(there, 0, core).start()

        @pl.when(role == 0)
        def _():
            half = lax.div(there, X)
            gj[z, half] = gall[there, y, core]
            panel_start(half)

    def meet(event):
        for way, piece in ((0, 0), (1, 1), (0, 1), (1, 0)):
            gy[event].recv(way, 0, piece)
        share(z_of(event), 1, core).start()
        share(z_of(event), 3, core).start()

    def close(event):
        gy[event].recv(0, 1, 0)
        gy[event].recv(1, 1, 1)
        share(z_of(event), 2, core).start()

    def multiply(event):
        there = z_of(event)
        landed(gall.at[there, :, other], gs_r.at[there])
        square[...] += jnp.dot(
            gj[there].reshape(ROWS, WIDE), gall[there].reshape(WIDE, WIDE), preferred_element_type=F32
        )

    def first(ring, step):
        ring.recv(0, step, 0)
        ring.recv(1, step, 1)

    def second(ring, step):
        ring.recv(0, step, 1)
        ring.recv(1, step, 0)

    def small(refs, slot, index, device):
        return remote(refs.at[slot], refs.at[slot], sent.at[10 + index], ss_r.at[index], device)

    square[...] = jnp.zeros_like(square)
    first(zr, 0)
    first(yr, 0)
    second(zr, 0)
    second(yr, 0)
    first(zr, 1)
    first(yr, 1)
    for event in (0, 1, 2):
        form(event)
    for event in (0, 1, 2):
        join(event)
    second(zr, 1)
    form(3)
    form(4)
    settle(0)
    first(zr, 2)
    settle(1)
    settle(2)
    join(3)
    join(4)
    second(zr, 2)
    form(5)
    form(6)
    spread(0)
    spread(1)
    spread(2)
    first(zr, 3)
    form(7)
    settle(3)
    join(5)
    settle(4)
    join(6)
    join(7)

    total = ss_z[0]
    for k in range(1, Z):
        total = total + ss_z[k]
    ss_y[y] = total
    for d in (1, 2, 3):
        small(ss_y, y, 0, at_y(wrap(y + d, Y))).start()

    meet(0)
    meet(1)
    spread(3)
    spread(4)
    meet(2)
    close(0)
    settle(5)
    settle(6)
    close(1)
    settle(7)

    landed(ss_y.at[pl.ds(0, 3)], ss_r.at[0])
    ss_x[x] = ss_y[0] + ss_y[1] + ss_y[2] + ss_y[3]
    for d in (1, 2, 3):
        small(ss_x, x, 1, at_x(wrap(x + d, X))).start()

    meet(3)
    close(2)
    spread(5)
    spread(6)
    meet(4)
    spread(7)
    close(3)
    close(4)

    landed(ss_x.at[pl.ds(0, 3)], ss_r.at[1])
    ss_c[core] = ss_x[0] + ss_x[1] + ss_x[2] + ss_x[3]
    small(ss_c, core, 2, sibling).start()

    meet(5)
    panel_wait(2)
    meet(6)
    meet(7)
    multiply(0)
    close(5)
    close(6)
    panel_wait(1)
    multiply(1)
    multiply(2)
    close(7)
    multiply(3)
    multiply(4)
    small(ss_c, other, 2, sibling).wait_recv()
    norm_total = (ss_c[0] + ss_c[1])[0:1, 0:1]
    factor = math.sqrt(FULL_ROWS) / (3.0 * (jnp.sqrt(norm_total) + norm_eps))
    factor_out[...] = jnp.broadcast_to(math.sqrt(FULL_COLS) * factor, factor_out.shape)
    panel_wait(3)
    multiply(5)
    multiply(6)
    panel_wait(4)
    multiply(7)

    pr = Ring(X, x, at_x, lambda b, p: pb.at[p, b, core], (0, 1), sent.at[8], pr_r)
    for half in (0, 1):
        gram = gj[z, half].astype(F32)
        tile = (
            cubic_coef * factor * factor * gram
            + quintic_coef * (factor * factor) * (factor * factor) * square[pl.ds(half * HALF, HALF)]
        )
        pb[half, x, core] = tile.astype(BF16)
    pr.start()

    def share_p(index, core_):
        place = pb.at[:, wrap(x + index, X), core_]
        return remote(place, place, sent.at[9], ps_r.at[index], sibling)

    def y_relay_copy(tile, side):
        return remote(
            up.at[tile, wrap(y + 2, Y), pl.ds(side * HALF, HALF)],
            y_relay.at[tile, side],
            sent.at[13],
            ur_r.at[tile, side],
            at_y(wrap(y + 1 - 2 * side, Y)),
        )

    def y_last_copy(tile, side, half):
        return remote(
            up.at[tile, wrap(y + 1 - 2 * side, Y), pl.ds(half * HALF, HALF)],
            y_last.at[tile, side, pl.ds(half * HALF, HALF)],
            sent.at[14],
            ul_r.at[tile, side, half],
            at_y(wrap(y + 1 - 2 * side, Y)),
        )

    def add_relay(tile):
        for side in (0, 1):
            y_relay_copy(tile, side).wait_recv()
            near = wrap(y + 1 - 2 * side, Y)
            place = pl.ds(side * HALF, HALF)
            up[tile, near, place] = up[tile, near, place] + y_relay[tile, side]
            y_last_copy(tile, side, side).start()

    def z_sum_copy(way, step, half):
        sign = 1 - 2 * way
        return remote(
            uz.at[wrap(z + sign * (4 - step), Z), pl.ds(half * HALF, HALF)],
            z_sum.at[way, step, half],
            sent.at[15],
            zs_r.at[way, step, half],
            at_z(wrap(z + sign, Z)),
        )

    def z_sum_step(step, second_half):
        for way in (0, 1):
            half = way if not second_half else 1 - way
            z_sum_copy(way, step, half).wait_recv()
            near = wrap(z + (1 - 2 * way) * (3 - step), Z)
            place = pl.ds(half * HALF, HALF)
            uz[near, place] = uz[near, place] + z_sum[way, step, half]
            z_sum_copy(way, step + 1, half).start()

    def grow(index):
        there = wrap(x + index, X)
        landed(pb.at[:, there, other], ps_r.at[index])
        for half in (0, 1):
            uz[there + half * X] = jnp.dot(
                pb[half, there].reshape(ROWS, WIDE),
                xa[:, :, pl.ds(SPLIT, TILE)].reshape(WIDE, TILE),
                preferred_element_type=F32,
            )
        if index == 2:
            for way in (0, 1):
                z_sum_copy(way, 0, way).start()
            for way in (0, 1):
                z_sum_copy(way, 1, 1 - way).start()
        for tile in range(TILES):
            columns = pl.ds(tile * TILE, TILE)
            term = lax.dot_general(
                pb[:, there].reshape(2 * ROWS, WIDE),
                jnp.concatenate([xb[there, :, columns], xb[there + X, :, columns]], axis=0),
                TN,
                preferred_element_type=F32,
            ).reshape(Y, ROWS, TILE)
            up[tile] = term if index == 0 else up[tile] + term
            if index == 2:
                for side in (0, 1):
                    y_relay_copy(tile, side).start()

    def begin_near(tile):
        for side in (0, 1):
            y_last_copy(tile, side, 1 - side).start()

    def finish_y(tile):
        for side in (0, 1):
            for half in (0, 1):
                y_last_copy(tile, side, half).wait_recv()
        columns = pl.ds(tile * TILE, TILE)
        product[:, columns] = (
            linear_coef * xb[z, :, columns].astype(F32) + up[tile, y] + y_last[tile, 0] + y_last[tile, 1]
        )

    def finish_z(half):
        for way in (0, 1):
            z_sum_copy(way, 3, half).wait_recv()
        rows, columns = pl.ds(half * HALF, HALF), pl.ds(SPLIT, TILE)
        product[rows, columns] = (
            linear_coef * xb[z, rows, columns].astype(F32)
            + uz[z, rows]
            + z_sum[0, 3, half]
            + z_sum[1, 3, half]
        )

    share_p(0, core).start()
    grow(0)
    first(pr, 0)
    second(pr, 0)
    share_p(1, core).start()
    share_p(3, core).start()
    grow(1)
    first(pr, 1)
    share_p(2, core).start()
    grow(3)
    grow(2)
    begin_near(0)
    begin_near(1)
    z_sum_step(0, False)
    add_relay(0)
    z_sum_step(1, True)
    add_relay(1)
    z_sum_step(1, False)
    z_sum_step(2, True)
    z_sum_step(2, False)
    finish_y(0)
    finish_y(1)
    finish_z(0)
    finish_z(1)

    for index, place in enumerate((
        xb.at[pl.ds(0, 7)],
        xa.at[pl.ds(0, 3)],
        part.at[:, 0],
        units.at[pl.ds(0, 5)],
        gj.at[pl.ds(0, 7)],
        gall.at[pl.ds(0, 3), pl.ds(0, 2), 0],
        gall.at[:, pl.ds(0, 3), 0],
        gall.at[:, :, 0],
        pb.at[0, pl.ds(0, 3)],
        pb.at[:, :, 0],
        ss_y.at[pl.ds(0, 3)],
        ss_x.at[pl.ds(0, 3)],
        ss_c.at[0],
        y_relay,
        y_last,
        uz.at[pl.ds(0, 7)],
    )):
        remote(place, place, sent.at[index], zr_r.at[0], sibling).wait_send()


def dma(*shape):
    return pltpu.SemaphoreType.DMA(shape)


def fused(momentum, gradient):
    vmem = pl.BlockSpec(memory_space=pltpu.VMEM)
    return pl.pallas_call(
        kernel,
        out_shape=(
            jax.ShapeDtypeStruct((ROWS, COLS), F32),
            jax.ShapeDtypeStruct((8, COLS), F32),
        ),
        in_specs=[vmem, vmem],
        out_specs=(vmem, vmem),
        scratch_shapes=[
            pltpu.VMEM((Y, ROWS, COLS), BF16),
            pltpu.VMEM((Z, ROWS, COLS), BF16),
            pltpu.VMEM((Z, 2, HALF, WIDE), F32),
            pltpu.VMEM((Z, HALF, WIDE), F32),
            pltpu.VMEM((Z, 6, UNIT, WIDE), F32),
            pltpu.VMEM((Z, 2, HALF, WIDE), BF16),
            pltpu.VMEM((Z, Y, 2, HALF, WIDE), BF16),
            pltpu.VMEM((2, X, 2, HALF, WIDE), BF16),
            pltpu.VMEM((TILES, Y, ROWS, TILE), F32),
            pltpu.VMEM((TILES, 2, HALF, TILE), F32),
            pltpu.VMEM((TILES, 2, ROWS, TILE), F32),
            pltpu.VMEM((Z, ROWS, TILE), F32),
            pltpu.VMEM((2, 4, 2, HALF, TILE), F32),
            pltpu.VMEM((ROWS, WIDE), F32),
            pltpu.VMEM((Z, 8, 128), F32),
            pltpu.VMEM((Y, 8, 128), F32),
            pltpu.VMEM((X, 8, 128), F32),
            pltpu.VMEM((2, 8, 128), F32),
            dma(16),
            dma(14),
            dma(6),
            dma(Z),
            dma(Z),
            dma(14),
            dma(Z),
            dma(Z, 6),
            dma(Z),
            dma(6),
            dma(X),
            dma(3),
            dma(TILES, 2),
            dma(TILES, 2, 2),
            dma(2, 4, 2),
        ],
        compiler_params=pltpu.CompilerParams(
            collective_id=0, has_side_effects=True, vmem_limit_bytes=56 * 1024 * 1024
        ),
    )(momentum, gradient)


def local(momentum, gradient):
    new_momentum = decay_rate * momentum + gradient.astype(F32)
    product, scale = fused(momentum, gradient)
    update = (scale * product.reshape(ROWS // 8, 8, COLS)).reshape(ROWS, COLS)
    return (new_momentum, update)


def solution(mesh):
    placed = (P("row", "col"), P("row", "col"))
    return jax.shard_map(
        local,
        mesh=mesh,
        in_specs=placed,
        out_specs=(P("row", "col"), P("row", "col")),
        check_vma=False,
    )
```

```python
import math

import jax
import jax.numpy as jnp
from jax import lax
from jax.experimental import pallas as pl
from jax.experimental.pallas import tpu as pltpu
from jax.sharding import PartitionSpec as P

decay_rate = 0.95
linear_coef = 3.4445
cubic_coef = -4.775
quintic_coef = 2.0315
norm_eps = 1e-07

X, Y, Z = 4, 4, 8
ROWS, COLS = 160, 1152
HALF = ROWS // 2
WIDE = Y * ROWS
UNIT = 16
EXTRA = pl.ds(UNIT, UNIT)
TILES = 2
TILE = COLS // 3
SPLIT = TILES * TILE
FULL_ROWS = ROWS * Y * Z
FULL_COLS = COLS * X * 2
NT = (((1,), (1,)), ((), ()))
TN = (((0,), (0,)), ((), ()))
F32 = jnp.float32
BF16 = jnp.bfloat16


def wrap(value, size):
    return lax.rem(value + size, size)


def remote(src, dst, send_sem, recv_sem, device):
    return pltpu.make_async_remote_copy(
        src_ref=src,
        dst_ref=dst,
        send_sem=send_sem,
        recv_sem=recv_sem,
        device_id=device,
        device_id_type=pl.DeviceIdType.MESH,
    )


class Ring:
    def __init__(self, size, position, device, region, last, send_sem, recv_sems):
        self.size, self.position, self.device = size, position, device
        self.region, self.last = region, last
        self.send_sem, self.recv_sems = send_sem, recv_sems
        self.slots = {}
        for way in (0, 1):
            for piece in range(len(last)):
                for step in range(size // 2 - (0 if last[piece] == way else 1)):
                    self.slots[way, step, piece] = len(self.slots)

    def copy(self, way, step, piece, block):
        sign = 1 - 2 * way
        place = self.region(block, piece)
        return remote(
            place,
            place,
            self.send_sem,
            self.recv_sems.at[self.slots[way, step, piece]],
            self.device(wrap(self.position + sign, self.size)),
        )

    def send(self, way, step, piece):
        sign = 1 - 2 * way
        self.copy(way, step, piece, wrap(self.position - sign * step, self.size)).start()

    def start(self):
        for way, piece in ((0, 0), (1, 1), (0, 1), (1, 0)):
            self.send(way, 0, piece)

    def recv(self, way, step, piece):
        if (way, step, piece) not in self.slots:
            return
        sign = 1 - 2 * way
        self.copy(way, step, piece, wrap(self.position - sign * (step + 1), self.size)).wait_recv()
        if (way, step + 1, piece) in self.slots:
            self.send(way, step + 1, piece)


OFFSETS = (0, 1, -1, 2, -2, 3, -3, 4)


def kernel(
    momentum,
    gradient,
    product,
    factor_out,
    xa, xb, part, sibling_part, units, gj, gall, pb, up, y_relay, y_last, uz, z_sum,
    square, ss_z, ss_y, ss_x, ss_c,
    sent, zr_r, yr_r, sp_r, us_r, gz_r, gt_r, gy_r, gs_r, pr_r, ps_r, ss_r, ur_r, ul_r, zs_r,
):
    row, col = lax.axis_index("row"), lax.axis_index("col")
    z, y = lax.div(row, Y), lax.rem(row, Y)
    x, core = lax.div(col, 2), lax.rem(col, 2)
    other = 1 - core

    def at_z(p):
        return (p * Y + y, col)

    def at_y(p):
        return (z * Y + p, col)

    def at_x(p):
        return (row, p * 2 + core)

    sibling = (row, x * 2 + other)

    barrier = pltpu.get_barrier_semaphore()
    partners = [at_z(wrap(z + d, Z)) for d in (1, -1, 2, -2)] + [sibling]
    partners += [at_y(wrap(y + d, Y)) for d in (1, 2, 3)]
    partners += [at_x(wrap(x + d, X)) for d in (1, 2, 3)]
    for partner in partners:
        pl.semaphore_signal(barrier, inc=1, device_id=partner, device_id_type=pl.DeviceIdType.MESH)
    iterate = (decay_rate * momentum[...] + gradient[...].astype(F32)).astype(BF16)
    xb[z] = iterate
    xa[y] = iterate
    pl.semaphore_wait(barrier, len(partners))

    zr = Ring(Z, z, at_z, lambda b, p: xb.at[b, pl.ds(p * HALF, HALF)], (0, 1), sent.at[0], zr_r)
    yr = Ring(Y, y, at_y, lambda b, p: xa.at[b, pl.ds(p * HALF, HALF)], (0, 1), sent.at[1], yr_r)
    for way, piece in ((0, 0), (1, 1), (0, 1), (1, 0)):
        zr.send(way, 0, piece)
        yr.send(way, 0, piece)

    def z_of(event):
        return wrap(z + OFFSETS[event], Z)

    def sibling_copy(there):
        return remote(
            part.at[there, other], sibling_part.at[there], sent.at[2], sp_r.at[there], sibling
        )

    def form(event):
        there = z_of(event)
        block = xb[there]
        part[there] = lax.dot_general(
            block, xa[...].reshape(WIDE, COLS), NT, preferred_element_type=F32
        ).reshape(2, HALF, WIDE)
        sibling_copy(there).start()
        wide = block.astype(F32)
        ss_z[there] = jnp.broadcast_to(jnp.sum(wide * wide, keepdims=True), (8, 128))

    def role_of(there):
        return wrap(x - lax.rem(there, X), X)

    def rows_of(unit):
        return pl.ds(pl.multiple_of(UNIT * (unit + lax.div(unit + 2, 3)), UNIT), UNIT)

    def unit_copy(there, d):
        to = wrap(x + d, X)
        return remote(
            part.at[there, core, rows_of(wrap(to - lax.rem(there, X), X))],
            units.at[there, d - 1],
            sent.at[3],
            us_r.at[there],
            at_x(to),
        )

    def extra_copy(there, slot):
        return remote(
            part.at[there, core, EXTRA],
            units.at[there, 3 + slot],
            sent.at[3],
            us_r.at[there],
            at_x(lax.rem(there, X)),
        )

    def join(event):
        there = z_of(event)
        sibling_copy(there).wait_recv()
        part[there, core] = part[there, core] + sibling_part[there]
        for d in (2, 1, 3):
            unit_copy(there, d).start()
        role = role_of(there)

        @pl.when(role != 0)
        def _():
            extra_copy(there, 3 - role).start()

    cut = ((0, 48), (48, 32))
    def panel_copy(way, hops, block, slot, piece):
        place = gj.at[block, piece]
        return remote(
            place, place, sent.at[4], gz_r.at[slot], at_z(wrap(z + (1 - 2 * way) * hops, Z))
        )

    def panel_start(piece):
        for hops in (2, 1):
            for way in (0, 1):
                panel_copy(way, hops, z, 4 * (hops - 1) + 2 * way + piece, piece).start()

    def panel_wait(distance):
        for way in (0, 1):
            for piece in (0, 1) if distance < 4 else (way,):
                slot = 4 * (distance - 1) + (2 * way + piece if distance < 4 else way)
                block = wrap(z - (1 - 2 * way) * distance, Z)
                panel_copy(way, 1, block, slot, piece).wait_recv()
                if distance == 2:
                    if piece == way:
                        panel_copy(way, 2, block, 12 + way, piece).start()
                    panel_copy(way, 1, block, 8 + 2 * way + piece, piece).start()

    gy = []
    for event in range(Z):
        there = z_of(event)
        gy.append(
            Ring(
                Y,
                y,
                at_y,
                lambda b, p, there=there: gall.at[there, b, core, pl.ds(*cut[p])],
                (0, 1),
                sent.at[6],
                gy_r.at[there],
            )
        )

    def tile_copy(there, d):
        place = gall.at[there, y, core, rows_of(role_of(there))]
        return remote(place, place, sent.at[5], gt_r.at[there], at_x(wrap(x + d, X)))

    def extra_tile_copy(there, d):
        place = gall.at[there, y, core, EXTRA]
        return remote(place, place, sent.at[5], gt_r.at[there], at_x(wrap(x + d, X)))

    def landed(place, sem):
        remote(place, place, sent.at[0], sem, sibling).wait_recv()

    def settle(event):
        there = z_of(event)
        role = role_of(there)
        rows = rows_of(role)

        @pl.when(role == 0)
        def _():
            landed(units.at[there], us_r.at[there])
            gall[there, y, core, EXTRA] = (
                part[there, core, EXTRA] + units[there, 3] + units[there, 4] + units[there, 5]
            ).astype(BF16)
            for d in (2, 1, 3):
                extra_tile_copy(there, d).start()

        @pl.when(role != 0)
        def _():
            landed(units.at[there, pl.ds(0, 3)], us_r.at[there])

        gall[there, y, core, rows] = (
            part[there, core, rows] + units[there, 0] + units[there, 1] + units[there, 2]
        ).astype(BF16)
        for d in (2, 1, 3):
            tile_copy(there, d).start()

    def share(there, k, core_):
        place = gall.at[there, wrap(y + k, Y), core_]
        return remote(place, place, sent.at[7], gs_r.at[there], sibling)

    def spread(event):
        there = z_of(event)
        role = role_of(there)
        @pl.when(role == 0)
        def _():
            landed(gall.at[there, y, core, pl.ds(0, 3 * UNIT)], gt_r.at[there])

        @pl.when(role != 0)
        def _():
            landed(gall.at[there, y, core, pl.ds(0, 4 * UNIT)], gt_r.at[there])

        gy[event].start()
        share(there, 0, core).start()

        @pl.when(role == 0)
        def _():
            half = lax.div(there, X)
            gj[z, half] = gall[there, y, core]
            panel_start(half)

    def meet(event):
        for way, piece in ((0, 0), (1, 1), (0, 1), (1, 0)):
            gy[event].recv(way, 0, piece)
        share(z_of(event), 1, core).start()
        share(z_of(event), 3, core).start()

    def close(event):
        gy[event].recv(0, 1, 0)
        gy[event].recv(1, 1, 1)
        share(z_of(event), 2, core).start()

    def multiply(event):
        there = z_of(event)
        landed(gall.at[there, :, other], gs_r.at[there])
        square[...] += jnp.dot(
            gj[there].reshape(ROWS, WIDE), gall[there].reshape(WIDE, WIDE), preferred_element_type=F32
        )

    def first(ring, step):
        ring.recv(0, step, 0)
        ring.recv(1, step, 1)

    def second(ring, step):
        ring.recv(0, step, 1)
        ring.recv(1, step, 0)

    def small(refs, slot, index, device):
        return remote(refs.at[slot], refs.at[slot], sent.at[10 + index], ss_r.at[index], device)

    square[...] = jnp.zeros_like(square)
    first(zr, 0)
    first(yr, 0)
    second(zr, 0)
    second(yr, 0)
    first(zr, 1)
    first(yr, 1)
    form(0)
    form(1)
    join(0)
    form(2)
    join(1)
    join(2)
    second(zr, 1)
    form(3)
    form(4)
    settle(0)
    join(3)
    first(zr, 2)
    settle(1)
    settle(2)
    join(4)
    second(zr, 2)
    form(5)
    form(6)
    spread(0)
    spread(1)
    settle(3)
    spread(2)
    first(zr, 3)
    form(7)
    join(5)
    settle(4)
    join(6)
    join(7)

    total = ss_z[0]
    for k in range(1, Z):
        total = total + ss_z[k]
    ss_y[y] = total
    for d in (1, 2, 3):
        small(ss_y, y, 0, at_y(wrap(y + d, Y))).start()

    meet(0)
    spread(3)
    meet(1)
    settle(5)
    spread(4)
    meet(2)
    close(0)
    settle(6)
    close(1)
    settle(7)
    meet(3)

    landed(ss_y.at[pl.ds(0, 3)], ss_r.at[0])
    ss_x[x] = ss_y[0] + ss_y[1] + ss_y[2] + ss_y[3]
    for d in (1, 2, 3):
        small(ss_x, x, 1, at_x(wrap(x + d, X))).start()

    spread(5)
    close(2)
    meet(4)
    spread(6)
    spread(7)
    close(3)

    landed(ss_x.at[pl.ds(0, 3)], ss_r.at[1])
    ss_c[core] = ss_x[0] + ss_x[1] + ss_x[2] + ss_x[3]
    small(ss_c, core, 2, sibling).start()

    close(4)
    meet(5)
    panel_wait(2)
    meet(6)
    meet(7)
    multiply(0)
    panel_wait(1)
    multiply(1)
    multiply(2)
    close(5)
    close(6)
    multiply(3)
    close(7)
    multiply(4)
    small(ss_c, other, 2, sibling).wait_recv()
    norm_total = (ss_c[0] + ss_c[1])[0:1, 0:1]
    factor = math.sqrt(FULL_ROWS) / (3.0 * (jnp.sqrt(norm_total) + norm_eps))
    factor_out[...] = jnp.broadcast_to(math.sqrt(FULL_COLS) * factor, factor_out.shape)
    panel_wait(3)
    multiply(5)
    multiply(6)
    panel_wait(4)
    multiply(7)

    pr = Ring(X, x, at_x, lambda b, p: pb.at[p, b, core], (0, 1), sent.at[8], pr_r)
    for half in (0, 1):
        gram = gj[z, half].astype(F32)
        tile = (
            cubic_coef * factor * factor * gram
            + quintic_coef * (factor * factor) * (factor * factor) * square[pl.ds(half * HALF, HALF)]
        )
        pb[half, x, core] = tile.astype(BF16)
    pr.start()

    def share_p(index, core_):
        place = pb.at[:, wrap(x + index, X), core_]
        return remote(place, place, sent.at[9], ps_r.at[index], sibling)

    def y_relay_copy(tile, side):
        return remote(
            up.at[tile, wrap(y + 2, Y), pl.ds(side * HALF, HALF)],
            y_relay.at[tile, side],
            sent.at[13],
            ur_r.at[tile, side],
            at_y(wrap(y + 1 - 2 * side, Y)),
        )

    def y_last_copy(tile, side, half):
        return remote(
            up.at[tile, wrap(y + 1 - 2 * side, Y), pl.ds(half * HALF, HALF)],
            y_last.at[tile, side, pl.ds(half * HALF, HALF)],
            sent.at[14],
            ul_r.at[tile, side, half],
            at_y(wrap(y + 1 - 2 * side, Y)),
        )

    def add_relay(tile):
        for side in (0, 1):
            y_relay_copy(tile, side).wait_recv()
            near = wrap(y + 1 - 2 * side, Y)
            place = pl.ds(side * HALF, HALF)
            up[tile, near, place] = up[tile, near, place] + y_relay[tile, side]
            y_last_copy(tile, side, side).start()

    def z_sum_copy(way, step, half):
        sign = 1 - 2 * way
        return remote(
            uz.at[wrap(z + sign * (4 - step), Z), pl.ds(half * HALF, HALF)],
            z_sum.at[way, step, half],
            sent.at[15],
            zs_r.at[way, step, half],
            at_z(wrap(z + sign, Z)),
        )

    def z_sum_step(step, second_half):
        for way in (0, 1):
            half = way if not second_half else 1 - way
            z_sum_copy(way, step, half).wait_recv()
            near = wrap(z + (1 - 2 * way) * (3 - step), Z)
            place = pl.ds(half * HALF, HALF)
            uz[near, place] = uz[near, place] + z_sum[way, step, half]
            z_sum_copy(way, step + 1, half).start()

    def grow(index):
        there = wrap(x + index, X)
        landed(pb.at[:, there, other], ps_r.at[index])
        for half in (0, 1):
            uz[there + half * X] = jnp.dot(
                pb[half, there].reshape(ROWS, WIDE),
                xa[:, :, pl.ds(SPLIT, TILE)].reshape(WIDE, TILE),
                preferred_element_type=F32,
            )
        if index == 2:
            for way in (0, 1):
                z_sum_copy(way, 0, way).start()
            for way in (0, 1):
                z_sum_copy(way, 1, 1 - way).start()
        for tile in range(TILES):
            columns = pl.ds(tile * TILE, TILE)
            term = lax.dot_general(
                pb[:, there].reshape(2 * ROWS, WIDE),
                jnp.concatenate([xb[there, :, columns], xb[there + X, :, columns]], axis=0),
                TN,
                preferred_element_type=F32,
            ).reshape(Y, ROWS, TILE)
            up[tile] = term if index == 0 else up[tile] + term
            if index == 2:
                for side in (0, 1):
                    y_relay_copy(tile, side).start()

    def begin_near(tile):
        for side in (0, 1):
            y_last_copy(tile, side, 1 - side).start()

    def finish_y(tile):
        for side in (0, 1):
            for half in (0, 1):
                y_last_copy(tile, side, half).wait_recv()
        columns = pl.ds(tile * TILE, TILE)
        product[:, columns] = (
            linear_coef * xb[z, :, columns].astype(F32) + up[tile, y] + y_last[tile, 0] + y_last[tile, 1]
        )

    def finish_z(half):
        for way in (0, 1):
            z_sum_copy(way, 3, half).wait_recv()
        rows, columns = pl.ds(half * HALF, HALF), pl.ds(SPLIT, TILE)
        product[rows, columns] = (
            linear_coef * xb[z, rows, columns].astype(F32)
            + uz[z, rows]
            + z_sum[0, 3, half]
            + z_sum[1, 3, half]
        )

    share_p(0, core).start()
    grow(0)
    first(pr, 0)
    second(pr, 0)
    share_p(1, core).start()
    share_p(3, core).start()
    grow(1)
    first(pr, 1)
    share_p(2, core).start()
    grow(3)
    grow(2)
    begin_near(0)
    begin_near(1)
    z_sum_step(0, False)
    add_relay(0)
    z_sum_step(1, True)
    add_relay(1)
    z_sum_step(1, False)
    z_sum_step(2, True)
    z_sum_step(2, False)
    finish_y(0)
    finish_y(1)
    finish_z(0)
    finish_z(1)

    for index, place in enumerate((
        xb.at[pl.ds(0, 7)],
        xa.at[pl.ds(0, 3)],
        part.at[:, 0],
        units.at[pl.ds(0, 5)],
        gj.at[pl.ds(0, 7)],
        gall.at[pl.ds(0, 3), pl.ds(0, 2), 0],
        gall.at[:, pl.ds(0, 3), 0],
        gall.at[:, :, 0],
        pb.at[0, pl.ds(0, 3)],
        pb.at[:, :, 0],
        ss_y.at[pl.ds(0, 3)],
        ss_x.at[pl.ds(0, 3)],
        ss_c.at[0],
        y_relay,
        y_last,
        uz.at[pl.ds(0, 7)],
    )):
        remote(place, place, sent.at[index], zr_r.at[0], sibling).wait_send()


def dma(*shape):
    return pltpu.SemaphoreType.DMA(shape)


def fused(momentum, gradient):
    vmem = pl.BlockSpec(memory_space=pltpu.VMEM)
    return pl.pallas_call(
        kernel,
        out_shape=(
            jax.ShapeDtypeStruct((ROWS, COLS), F32),
            jax.ShapeDtypeStruct((8, COLS), F32),
        ),
        in_specs=[vmem, vmem],
        out_specs=(vmem, vmem),
        scratch_shapes=[
            pltpu.VMEM((Y, ROWS, COLS), BF16),
            pltpu.VMEM((Z, ROWS, COLS), BF16),
            pltpu.VMEM((Z, 2, HALF, WIDE), F32),
            pltpu.VMEM((Z, HALF, WIDE), F32),
            pltpu.VMEM((Z, 6, UNIT, WIDE), F32),
            pltpu.VMEM((Z, 2, HALF, WIDE), BF16),
            pltpu.VMEM((Z, Y, 2, HALF, WIDE), BF16),
            pltpu.VMEM((2, X, 2, HALF, WIDE), BF16),
            pltpu.VMEM((TILES, Y, ROWS, TILE), F32),
            pltpu.VMEM((TILES, 2, HALF, TILE), F32),
            pltpu.VMEM((TILES, 2, ROWS, TILE), F32),
            pltpu.VMEM((Z, ROWS, TILE), F32),
            pltpu.VMEM((2, 4, 2, HALF, TILE), F32),
            pltpu.VMEM((ROWS, WIDE), F32),
            pltpu.VMEM((Z, 8, 128), F32),
            pltpu.VMEM((Y, 8, 128), F32),
            pltpu.VMEM((X, 8, 128), F32),
            pltpu.VMEM((2, 8, 128), F32),
            dma(16),
            dma(14),
            dma(6),
            dma(Z),
            dma(Z),
            dma(14),
            dma(Z),
            dma(Z, 6),
            dma(Z),
            dma(6),
            dma(X),
            dma(3),
            dma(TILES, 2),
            dma(TILES, 2, 2),
            dma(2, 4, 2),
        ],
        compiler_params=pltpu.CompilerParams(
            collective_id=0, has_side_effects=True, vmem_limit_bytes=56 * 1024 * 1024
        ),
    )(momentum, gradient)


def local(momentum, gradient):
    new_momentum = decay_rate * momentum + gradient.astype(F32)
    product, scale = fused(momentum, gradient)
    update = (scale * product.reshape(ROWS // 8, 8, COLS)).reshape(ROWS, COLS)
    return (new_momentum, update)


def solution(mesh):
    placed = (P("row", "col"), P("row", "col"))
    return jax.shard_map(
        local,
        mesh=mesh,
        in_specs=placed,
        out_specs=(P("row", "col"), P("row", "col")),
        check_vma=False,
    )
```

```python
import math

import jax
import jax.numpy as jnp
from jax import lax
from jax.experimental import pallas as pl
from jax.experimental.pallas import tpu as pltpu
from jax.sharding import PartitionSpec as P

decay_rate = 0.95
linear_coef = 3.4445
cubic_coef = -4.775
quintic_coef = 2.0315
norm_eps = 1e-07

X, Y, Z = 4, 4, 8
ROWS, COLS = 160, 1152
HALF = ROWS // 2
WIDE = Y * ROWS
UNIT = 16
EXTRA = pl.ds(UNIT, UNIT)
TILES = 2
TILE = COLS // 3
SPLIT = TILES * TILE
FULL_ROWS = ROWS * Y * Z
FULL_COLS = COLS * X * 2
NT = (((1,), (1,)), ((), ()))
TN = (((0,), (0,)), ((), ()))
F32 = jnp.float32
BF16 = jnp.bfloat16


def wrap(value, size):
    return lax.rem(value + size, size)


def remote(src, dst, send_sem, recv_sem, device):
    return pltpu.make_async_remote_copy(
        src_ref=src,
        dst_ref=dst,
        send_sem=send_sem,
        recv_sem=recv_sem,
        device_id=device,
        device_id_type=pl.DeviceIdType.MESH,
    )


class Ring:
    def __init__(self, size, position, device, region, last, send_sem, recv_sems):
        self.size, self.position, self.device = size, position, device
        self.region, self.last = region, last
        self.send_sem, self.recv_sems = send_sem, recv_sems
        self.slots = {}
        for way in (0, 1):
            for piece in range(len(last)):
                for step in range(size // 2 - (0 if last[piece] == way else 1)):
                    self.slots[way, step, piece] = len(self.slots)

    def copy(self, way, step, piece, block):
        sign = 1 - 2 * way
        place = self.region(block, piece)
        return remote(
            place,
            place,
            self.send_sem,
            self.recv_sems.at[self.slots[way, step, piece]],
            self.device(wrap(self.position + sign, self.size)),
        )

    def send(self, way, step, piece):
        sign = 1 - 2 * way
        self.copy(way, step, piece, wrap(self.position - sign * step, self.size)).start()

    def start(self):
        for way, piece in ((0, 0), (1, 1), (0, 1), (1, 0)):
            self.send(way, 0, piece)

    def recv(self, way, step, piece):
        if (way, step, piece) not in self.slots:
            return
        sign = 1 - 2 * way
        self.copy(way, step, piece, wrap(self.position - sign * (step + 1), self.size)).wait_recv()
        if (way, step + 1, piece) in self.slots:
            self.send(way, step + 1, piece)


OFFSETS = (0, 1, -1, 2, -2, 3, -3, 4)


def kernel(
    momentum,
    gradient,
    product,
    factor_out,
    xa, xb, part, sibling_part, units, gj, gall, pb, up, y_relay, y_last, uz, z_sum,
    square, ss_z, ss_y, ss_x, ss_c,
    sent, zr_r, yr_r, sp_r, us_r, gz_r, gt_r, gy_r, gs_r, pr_r, ps_r, ss_r, ur_r, ul_r, zs_r,
):
    row, col = lax.axis_index("row"), lax.axis_index("col")
    z, y = lax.div(row, Y), lax.rem(row, Y)
    x, core = lax.div(col, 2), lax.rem(col, 2)
    other = 1 - core

    def at_z(p):
        return (p * Y + y, col)

    def at_y(p):
        return (z * Y + p, col)

    def at_x(p):
        return (row, p * 2 + core)

    sibling = (row, x * 2 + other)

    barrier = pltpu.get_barrier_semaphore()
    partners = [at_z(wrap(z + d, Z)) for d in (1, -1, 2, -2)] + [sibling]
    partners += [at_y(wrap(y + d, Y)) for d in (1, 2, 3)]
    partners += [at_x(wrap(x + d, X)) for d in (1, 2, 3)]
    for partner in partners:
        pl.semaphore_signal(barrier, inc=1, device_id=partner, device_id_type=pl.DeviceIdType.MESH)
    iterate = (decay_rate * momentum[...] + gradient[...].astype(F32)).astype(BF16)
    xb[z] = iterate
    xa[y] = iterate
    pl.semaphore_wait(barrier, len(partners))

    zr = Ring(Z, z, at_z, lambda b, p: xb.at[b, pl.ds(p * HALF, HALF)], (0, 1), sent.at[0], zr_r)
    yr = Ring(Y, y, at_y, lambda b, p: xa.at[b, pl.ds(p * HALF, HALF)], (0, 1), sent.at[1], yr_r)
    for way, piece in ((0, 0), (1, 1), (0, 1), (1, 0)):
        zr.send(way, 0, piece)
        yr.send(way, 0, piece)

    def z_of(event):
        return wrap(z + OFFSETS[event], Z)

    def sibling_copy(there):
        return remote(
            part.at[there, other], sibling_part.at[there], sent.at[2], sp_r.at[there], sibling
        )

    def form(event):
        there = z_of(event)
        block = xb[there]
        part[there] = lax.dot_general(
            block, xa[...].reshape(WIDE, COLS), NT, preferred_element_type=F32
        ).reshape(2, HALF, WIDE)
        sibling_copy(there).start()
        wide = block.astype(F32)
        ss_z[there] = jnp.broadcast_to(jnp.sum(wide * wide, keepdims=True), (8, 128))

    def role_of(there):
        return wrap(x - lax.rem(there, X), X)

    def rows_of(unit):
        return pl.ds(pl.multiple_of(UNIT * (unit + lax.div(unit + 2, 3)), UNIT), UNIT)

    def unit_copy(there, d):
        to = wrap(x + d, X)
        return remote(
            part.at[there, core, rows_of(wrap(to - lax.rem(there, X), X))],
            units.at[there, d - 1],
            sent.at[3],
            us_r.at[there],
            at_x(to),
        )

    def extra_copy(there, slot):
        return remote(
            part.at[there, core, EXTRA],
            units.at[there, 3 + slot],
            sent.at[3],
            us_r.at[there],
            at_x(lax.rem(there, X)),
        )

    def join(event):
        there = z_of(event)
        sibling_copy(there).wait_recv()
        part[there, core] = part[there, core] + sibling_part[there]
        for d in (2, 1, 3):
            unit_copy(there, d).start()
        role = role_of(there)

        @pl.when(role != 0)
        def _():
            extra_copy(there, 3 - role).start()

    cut = ((0, 48), (48, 32))
    def panel_copy(way, hops, block, slot, piece):
        place = gj.at[block, piece]
        return remote(
            place, place, sent.at[4], gz_r.at[slot], at_z(wrap(z + (1 - 2 * way) * hops, Z))
        )

    def panel_start(piece):
        for hops in (2, 1):
            for way in (0, 1):
                panel_copy(way, hops, z, 4 * (hops - 1) + 2 * way + piece, piece).start()

    def panel_wait(distance):
        for way in (0, 1):
            for piece in (0, 1) if distance < 4 else (way,):
                slot = 4 * (distance - 1) + (2 * way + piece if distance < 4 else way)
                block = wrap(z - (1 - 2 * way) * distance, Z)
                panel_copy(way, 1, block, slot, piece).wait_recv()
                if distance == 2:
                    if piece == way:
                        panel_copy(way, 2, block, 12 + way, piece).start()
                    panel_copy(way, 1, block, 8 + 2 * way + piece, piece).start()

    gy = []
    for event in range(Z):
        there = z_of(event)
        gy.append(
            Ring(
                Y,
                y,
                at_y,
                lambda b, p, there=there: gall.at[there, b, core, pl.ds(*cut[p])],
                (0, 1),
                sent.at[6],
                gy_r.at[there],
            )
        )

    def tile_copy(there, d):
        place = gall.at[there, y, core, rows_of(role_of(there))]
        return remote(place, place, sent.at[5], gt_r.at[there], at_x(wrap(x + d, X)))

    def extra_tile_copy(there, d):
        place = gall.at[there, y, core, EXTRA]
        return remote(place, place, sent.at[5], gt_r.at[there], at_x(wrap(x + d, X)))

    def landed(place, sem):
        remote(place, place, sent.at[0], sem, sibling).wait_recv()

    def settle(event):
        there = z_of(event)
        role = role_of(there)
        rows = rows_of(role)

        @pl.when(role == 0)
        def _():
            landed(units.at[there], us_r.at[there])
            gall[there, y, core, EXTRA] = (
                part[there, core, EXTRA] + units[there, 3] + units[there, 4] + units[there, 5]
            ).astype(BF16)
            for d in (2, 1, 3):
                extra_tile_copy(there, d).start()

        @pl.when(role != 0)
        def _():
            landed(units.at[there, pl.ds(0, 3)], us_r.at[there])

        gall[there, y, core, rows] = (
            part[there, core, rows] + units[there, 0] + units[there, 1] + units[there, 2]
        ).astype(BF16)
        for d in (2, 1, 3):
            tile_copy(there, d).start()

    def share(there, k, core_):
        place = gall.at[there, wrap(y + k, Y), core_]
        return remote(place, place, sent.at[7], gs_r.at[there], sibling)

    def spread(event):
        there = z_of(event)
        role = role_of(there)
        @pl.when(role == 0)
        def _():
            landed(gall.at[there, y, core, pl.ds(0, 3 * UNIT)], gt_r.at[there])

        @pl.when(role != 0)
        def _():
            landed(gall.at[there, y, core, pl.ds(0, 4 * UNIT)], gt_r.at[there])

        gy[event].start()
        share(there, 0, core).start()

        @pl.when(role == 0)
        def _():
            half = lax.div(there, X)
            gj[z, half] = gall[there, y, core]
            panel_start(half)

    def meet(event):
        for way, piece in ((0, 0), (1, 1), (0, 1), (1, 0)):
            gy[event].recv(way, 0, piece)
        share(z_of(event), 1, core).start()
        share(z_of(event), 3, core).start()

    def close(event):
        gy[event].recv(0, 1, 0)
        gy[event].recv(1, 1, 1)
        share(z_of(event), 2, core).start()

    def multiply(event):
        there = z_of(event)
        landed(gall.at[there, :, other], gs_r.at[there])
        square[...] += jnp.dot(
            gj[there].reshape(ROWS, WIDE), gall[there].reshape(WIDE, WIDE), preferred_element_type=F32
        )

    def first(ring, step):
        ring.recv(0, step, 0)
        ring.recv(1, step, 1)

    def second(ring, step):
        ring.recv(0, step, 1)
        ring.recv(1, step, 0)

    def small(refs, slot, index, device):
        return remote(refs.at[slot], refs.at[slot], sent.at[10 + index], ss_r.at[index], device)

    square[...] = jnp.zeros_like(square)
    first(zr, 0)
    first(yr, 0)
    second(zr, 0)
    second(yr, 0)
    first(zr, 1)
    first(yr, 1)
    form(0)
    form(1)
    join(0)
    form(2)
    join(1)
    join(2)
    second(zr, 1)
    form(3)
    form(4)
    settle(0)
    join(3)
    first(zr, 2)
    settle(1)
    settle(2)
    join(4)
    second(zr, 2)
    spread(0)
    form(5)
    form(6)
    spread(1)
    join(5)
    settle(3)
    spread(2)
    join(6)
    first(zr, 3)
    form(7)
    settle(4)
    join(7)

    total = ss_z[0]
    for k in range(1, Z):
        total = total + ss_z[k]
    ss_y[y] = total
    for d in (1, 2, 3):
        small(ss_y, y, 0, at_y(wrap(y + d, Y))).start()

    meet(0)
    meet(1)
    spread(3)
    settle(5)
    meet(2)
    settle(6)
    spread(4)
    settle(7)
    spread(5)
    meet(3)
    spread(6)
    spread(7)
    meet(4)

    landed(ss_y.at[pl.ds(0, 3)], ss_r.at[0])
    ss_x[x] = ss_y[0] + ss_y[1] + ss_y[2] + ss_y[3]
    for d in (1, 2, 3):
        small(ss_x, x, 1, at_x(wrap(x + d, X))).start()

    close(0)
    close(1)
    close(2)
    meet(5)
    panel_wait(2)
    meet(6)
    meet(7)

    landed(ss_x.at[pl.ds(0, 3)], ss_r.at[1])
    ss_c[core] = ss_x[0] + ss_x[1] + ss_x[2] + ss_x[3]
    small(ss_c, core, 2, sibling).start()

    close(3)
    close(4)
    multiply(0)
    close(5)
    panel_wait(1)
    multiply(1)
    multiply(2)
    close(6)
    multiply(3)
    close(7)
    multiply(4)
    small(ss_c, other, 2, sibling).wait_recv()
    norm_total = (ss_c[0] + ss_c[1])[0:1, 0:1]
    factor = math.sqrt(FULL_ROWS) / (3.0 * (jnp.sqrt(norm_total) + norm_eps))
    factor_out[...] = jnp.broadcast_to(math.sqrt(FULL_COLS) * factor, factor_out.shape)
    panel_wait(3)
    multiply(5)
    multiply(6)
    panel_wait(4)
    multiply(7)

    pr = Ring(X, x, at_x, lambda b, p: pb.at[p, b, core], (0, 1), sent.at[8], pr_r)
    for half in (0, 1):
        gram = gj[z, half].astype(F32)
        tile = (
            cubic_coef * factor * factor * gram
            + quintic_coef * (factor * factor) * (factor * factor) * square[pl.ds(half * HALF, HALF)]
        )
        pb[half, x, core] = tile.astype(BF16)
    pr.start()

    def share_p(index, core_):
        place = pb.at[:, wrap(x + index, X), core_]
        return remote(place, place, sent.at[9], ps_r.at[index], sibling)

    def y_relay_copy(tile, side):
        return remote(
            up.at[tile, wrap(y + 2, Y), pl.ds(side * HALF, HALF)],
            y_relay.at[tile, side],
            sent.at[13],
            ur_r.at[tile, side],
            at_y(wrap(y + 1 - 2 * side, Y)),
        )

    def y_last_copy(tile, side, half):
        return remote(
            up.at[tile, wrap(y + 1 - 2 * side, Y), pl.ds(half * HALF, HALF)],
            y_last.at[tile, side, pl.ds(half * HALF, HALF)],
            sent.at[14],
            ul_r.at[tile, side, half],
            at_y(wrap(y + 1 - 2 * side, Y)),
        )

    def add_relay(tile):
        for side in (0, 1):
            y_relay_copy(tile, side).wait_recv()
            near = wrap(y + 1 - 2 * side, Y)
            place = pl.ds(side * HALF, HALF)
            up[tile, near, place] = up[tile, near, place] + y_relay[tile, side]
            y_last_copy(tile, side, side).start()

    def z_sum_copy(way, step, half):
        sign = 1 - 2 * way
        return remote(
            uz.at[wrap(z + sign * (4 - step), Z), pl.ds(half * HALF, HALF)],
            z_sum.at[way, step, half],
            sent.at[15],
            zs_r.at[way, step, half],
            at_z(wrap(z + sign, Z)),
        )

    def z_sum_step(step, second_half):
        for way in (0, 1):
            half = way if not second_half else 1 - way
            z_sum_copy(way, step, half).wait_recv()
            near = wrap(z + (1 - 2 * way) * (3 - step), Z)
            place = pl.ds(half * HALF, HALF)
            uz[near, place] = uz[near, place] + z_sum[way, step, half]
            z_sum_copy(way, step + 1, half).start()

    def grow(index):
        there = wrap(x + index, X)
        landed(pb.at[:, there, other], ps_r.at[index])
        for half in (0, 1):
            uz[there + half * X] = jnp.dot(
                pb[half, there].reshape(ROWS, WIDE),
                xa[:, :, pl.ds(SPLIT, TILE)].reshape(WIDE, TILE),
                preferred_element_type=F32,
            )
        if index == 2:
            for way in (0, 1):
                z_sum_copy(way, 0, way).start()
            for way in (0, 1):
                z_sum_copy(way, 1, 1 - way).start()
        for tile in range(TILES):
            columns = pl.ds(tile * TILE, TILE)
            term = lax.dot_general(
                pb[:, there].reshape(2 * ROWS, WIDE),
                jnp.concatenate([xb[there, :, columns], xb[there + X, :, columns]], axis=0),
                TN,
                preferred_element_type=F32,
            ).reshape(Y, ROWS, TILE)
            up[tile] = term if index == 0 else up[tile] + term
            if index == 2:
                for side in (0, 1):
                    y_relay_copy(tile, side).start()

    def begin_near(tile):
        for side in (0, 1):
            y_last_copy(tile, side, 1 - side).start()

    def finish_y(tile):
        for side in (0, 1):
            for half in (0, 1):
                y_last_copy(tile, side, half).wait_recv()
        columns = pl.ds(tile * TILE, TILE)
        product[:, columns] = (
            linear_coef * xb[z, :, columns].astype(F32) + up[tile, y] + y_last[tile, 0] + y_last[tile, 1]
        )

    def finish_z(half):
        for way in (0, 1):
            z_sum_copy(way, 3, half).wait_recv()
        rows, columns = pl.ds(half * HALF, HALF), pl.ds(SPLIT, TILE)
        product[rows, columns] = (
            linear_coef * xb[z, rows, columns].astype(F32)
            + uz[z, rows]
            + z_sum[0, 3, half]
            + z_sum[1, 3, half]
        )

    share_p(0, core).start()
    grow(0)
    first(pr, 0)
    second(pr, 0)
    share_p(1, core).start()
    share_p(3, core).start()
    grow(1)
    first(pr, 1)
    share_p(2, core).start()
    grow(3)
    grow(2)
    begin_near(0)
    begin_near(1)
    z_sum_step(0, False)
    add_relay(0)
    z_sum_step(1, True)
    add_relay(1)
    z_sum_step(1, False)
    z_sum_step(2, True)
    z_sum_step(2, False)
    finish_y(0)
    finish_y(1)
    finish_z(0)
    finish_z(1)

    for index, place in enumerate((
        xb.at[pl.ds(0, 7)],
        xa.at[pl.ds(0, 3)],
        part.at[:, 0],
        units.at[pl.ds(0, 5)],
        gj.at[pl.ds(0, 7)],
        gall.at[pl.ds(0, 3), pl.ds(0, 2), 0],
        gall.at[:, pl.ds(0, 3), 0],
        gall.at[:, :, 0],
        pb.at[0, pl.ds(0, 3)],
        pb.at[:, :, 0],
        ss_y.at[pl.ds(0, 3)],
        ss_x.at[pl.ds(0, 3)],
        ss_c.at[0],
        y_relay,
        y_last,
        uz.at[pl.ds(0, 7)],
    )):
        remote(place, place, sent.at[index], zr_r.at[0], sibling).wait_send()


def dma(*shape):
    return pltpu.SemaphoreType.DMA(shape)


def fused(momentum, gradient):
    vmem = pl.BlockSpec(memory_space=pltpu.VMEM)
    return pl.pallas_call(
        kernel,
        out_shape=(
            jax.ShapeDtypeStruct((ROWS, COLS), F32),
            jax.ShapeDtypeStruct((8, COLS), F32),
        ),
        in_specs=[vmem, vmem],
        out_specs=(vmem, vmem),
        scratch_shapes=[
            pltpu.VMEM((Y, ROWS, COLS), BF16),
            pltpu.VMEM((Z, ROWS, COLS), BF16),
            pltpu.VMEM((Z, 2, HALF, WIDE), F32),
            pltpu.VMEM((Z, HALF, WIDE), F32),
            pltpu.VMEM((Z, 6, UNIT, WIDE), F32),
            pltpu.VMEM((Z, 2, HALF, WIDE), BF16),
            pltpu.VMEM((Z, Y, 2, HALF, WIDE), BF16),
            pltpu.VMEM((2, X, 2, HALF, WIDE), BF16),
            pltpu.VMEM((TILES, Y, ROWS, TILE), F32),
            pltpu.VMEM((TILES, 2, HALF, TILE), F32),
            pltpu.VMEM((TILES, 2, ROWS, TILE), F32),
            pltpu.VMEM((Z, ROWS, TILE), F32),
            pltpu.VMEM((2, 4, 2, HALF, TILE), F32),
            pltpu.VMEM((ROWS, WIDE), F32),
            pltpu.VMEM((Z, 8, 128), F32),
            pltpu.VMEM((Y, 8, 128), F32),
            pltpu.VMEM((X, 8, 128), F32),
            pltpu.VMEM((2, 8, 128), F32),
            dma(16),
            dma(14),
            dma(6),
            dma(Z),
            dma(Z),
            dma(14),
            dma(Z),
            dma(Z, 6),
            dma(Z),
            dma(6),
            dma(X),
            dma(3),
            dma(TILES, 2),
            dma(TILES, 2, 2),
            dma(2, 4, 2),
        ],
        compiler_params=pltpu.CompilerParams(
            collective_id=0, has_side_effects=True, vmem_limit_bytes=56 * 1024 * 1024
        ),
    )(momentum, gradient)


def local(momentum, gradient):
    new_momentum = decay_rate * momentum + gradient.astype(F32)
    product, scale = fused(momentum, gradient)
    update = (scale * product.reshape(ROWS // 8, 8, COLS)).reshape(ROWS, COLS)
    return (new_momentum, update)


def solution(mesh):
    placed = (P("row", "col"), P("row", "col"))
    return jax.shard_map(
        local,
        mesh=mesh,
        in_specs=placed,
        out_specs=(P("row", "col"), P("row", "col")),
        check_vma=False,
    )
```

```python
import math

import jax
import jax.numpy as jnp
from jax import lax
from jax.experimental import pallas as pl
from jax.experimental.pallas import tpu as pltpu
from jax.sharding import PartitionSpec as P

decay_rate = 0.95
linear_coef = 3.4445
cubic_coef = -4.775
quintic_coef = 2.0315
norm_eps = 1e-07

X, Y, Z = 4, 4, 8
ROWS, COLS = 160, 1152
HALF = ROWS // 2
WIDE = Y * ROWS
UNIT = 16
EXTRA = pl.ds(UNIT, UNIT)
TILES = 2
TILE = COLS // 3
SPLIT = TILES * TILE
FULL_ROWS = ROWS * Y * Z
FULL_COLS = COLS * X * 2
NT = (((1,), (1,)), ((), ()))
TN = (((0,), (0,)), ((), ()))
F32 = jnp.float32
BF16 = jnp.bfloat16


def wrap(value, size):
    return lax.rem(value + size, size)


def remote(src, dst, send_sem, recv_sem, device):
    return pltpu.make_async_remote_copy(
        src_ref=src,
        dst_ref=dst,
        send_sem=send_sem,
        recv_sem=recv_sem,
        device_id=device,
        device_id_type=pl.DeviceIdType.MESH,
    )


class Ring:
    def __init__(self, size, position, device, region, whole, send_sem, recv_sems):
        self.size, self.position, self.device = size, position, device
        self.region, self.whole = region, whole
        self.send_sem, self.recv_sems = send_sem, recv_sems

    def send(self, kind, step):
        for way in (0, 1):
            sign = 1 - 2 * way
            place = self.region(
                wrap(self.position - sign * step, self.size), way if kind == 0 else 1 - way
            )
            remote(
                place,
                place,
                self.send_sem,
                self.recv_sems.at[2 * step + kind],
                self.device(wrap(self.position + sign, self.size)),
            ).start()

    def start(self):
        self.send(0, 0)
        self.send(1, 0)

    def recv(self, kind, step):
        remote(
            self.whole, self.whole, self.send_sem, self.recv_sems.at[2 * step + kind], self.device(self.position)
        ).wait_recv()
        if step + 1 < self.size // 2 - kind:
            self.send(kind, step + 1)


OFFSETS = (0, 1, -1, 2, -2, 3, -3, 4)


def kernel(
    momentum,
    gradient,
    product,
    factor_out,
    momentum_here, gradient_here, load_sems, xa, xb, part, sibling_part, units, gj, gall, pb, up, y_relay, y_last, uz, z_sum,
    square, ss_z, ss_y, ss_x, ss_c,
    sent, zr_r, yr_r, sp_r, us_r, gz_r, gt_r, gy_r, gs_r, pr_r, ps_r, ss_r, ur_r, ul_r, zs_r,
):
    row, col = lax.axis_index("row"), lax.axis_index("col")
    z, y = lax.div(row, Y), lax.rem(row, Y)
    x, core = lax.div(col, 2), lax.rem(col, 2)
    other = 1 - core

    def at_z(p):
        return (p * Y + y, col)

    def at_y(p):
        return (z * Y + p, col)

    def at_x(p):
        return (row, p * 2 + core)

    sibling = (row, x * 2 + other)

    barrier = pltpu.get_barrier_semaphore()
    partners = [at_z(wrap(z + d, Z)) for d in (1, -1, 2, -2)] + [sibling]
    partners += [at_y(wrap(y + d, Y)) for d in (1, 2, 3)]
    partners += [at_x(wrap(x + d, X)) for d in (1, 2, 3)]
    for partner in partners:
        pl.semaphore_signal(barrier, inc=1, device_id=partner, device_id_type=pl.DeviceIdType.MESH)
    loads = [
        pltpu.make_async_copy(momentum, momentum_here, load_sems.at[0]),
        pltpu.make_async_copy(gradient, gradient_here, load_sems.at[1]),
    ]
    for copy in loads:
        copy.start()
    for copy in loads:
        copy.wait()
    iterate = (decay_rate * momentum_here[...] + gradient_here[...].astype(F32)).astype(BF16)
    xb[z] = iterate
    xa[y] = iterate
    pl.semaphore_wait(barrier, len(partners))

    zr = Ring(Z, z, at_z, lambda b, p: xb.at[b, pl.ds(p * HALF, HALF)], xb.at[0], sent.at[0], zr_r)
    yr = Ring(Y, y, at_y, lambda b, p: xa.at[b, pl.ds(p * HALF, HALF)], xa.at[0], sent.at[1], yr_r)
    for kind in (0, 1):
        zr.send(kind, 0)
        yr.send(kind, 0)

    def z_of(event):
        return wrap(z + OFFSETS[event], Z)

    def sibling_copy(there):
        return remote(
            part.at[there, other], sibling_part.at[there], sent.at[2], sp_r.at[there], sibling
        )

    def form(event):
        there = z_of(event)
        block = xb[there]
        part[there] = lax.dot_general(
            block, xa[...].reshape(WIDE, COLS), NT, preferred_element_type=F32
        ).reshape(2, HALF, WIDE)
        sibling_copy(there).start()
        wide = block.astype(F32)
        ss_z[there] = jnp.broadcast_to(jnp.sum(wide * wide, keepdims=True), (8, 128))

    def role_of(there):
        return wrap(x - lax.rem(there, X), X)

    def rows_of(unit):
        return pl.ds(pl.multiple_of(UNIT * (unit + lax.div(unit + 2, 3)), UNIT), UNIT)

    def unit_copy(there, d):
        to = wrap(x + d, X)
        return remote(
            part.at[there, core, rows_of(wrap(to - lax.rem(there, X), X))],
            units.at[there, d - 1],
            sent.at[3],
            us_r.at[there],
            at_x(to),
        )

    def extra_copy(there, slot):
        return remote(
            part.at[there, core, EXTRA],
            units.at[there, 3 + slot],
            sent.at[3],
            us_r.at[there],
            at_x(lax.rem(there, X)),
        )

    def join(event):
        there = z_of(event)
        sibling_copy(there).wait_recv()
        part[there, core] = part[there, core] + sibling_part[there]
        for d in (2, 1, 3):
            unit_copy(there, d).start()
        role = role_of(there)

        @pl.when(role != 0)
        def _():
            extra_copy(there, 3 - role).start()

    cut = ((0, 48), (48, 32))
    def panel_copy(way, hops, block, slot, piece):
        place = gj.at[block, piece]
        return remote(
            place, place, sent.at[4], gz_r.at[slot], at_z(wrap(z + (1 - 2 * way) * hops, Z))
        )

    def panel_start(piece, late):
        for hops in (2, 1):
            for way in (0, 1):
                slot = 0 if hops == 1 else 4 + 2 * way + late
                panel_copy(way, hops, z, slot, piece).start()

    def panel_on(late):
        for way in (0, 1):
            block = wrap(z - (1 - 2 * way) * 2, Z)
            near = lax.div(wrap(wrap(x - block, Z) + 1 - Z, Z), X)
            middle = wrap(wrap(x - block, Z) - Z, X) == 2

            def go(piece, slot):
                landed(gj.at[0, 0], gz_r.at[slot])

                @pl.when(piece == way)
                def _():
                    panel_copy(way, 2, block, 3, piece).start()

                panel_copy(way, 1, block, 2, piece).start()

            @pl.when(middle if late else jnp.logical_not(middle))
            def _():
                go(near, 4 + 2 * way)

            if late:
                go(1 - near, 5 + 2 * way)

    def panel_wait(distance):
        landed(gj.at[pl.ds(0, 2)] if distance < 4 else gj.at[0], gz_r.at[distance - 1])

    gy = []
    for event in range(Z):
        there = z_of(event)
        gy.append(
            Ring(
                Y,
                y,
                at_y,
                lambda b, p, there=there: gall.at[there, b, core, pl.ds(*cut[p])],
                gall.at[there, 0, core],
                sent.at[6],
                gy_r.at[there],
            )
        )

    def tile_copy(there, d):
        place = gall.at[there, y, core, rows_of(role_of(there))]
        return remote(place, place, sent.at[5], gt_r.at[there], at_x(wrap(x + d, X)))

    def extra_tile_copy(there, d):
        place = gall.at[there, y, core, EXTRA]
        return remote(place, place, sent.at[5], gt_r.at[there], at_x(wrap(x + d, X)))

    def landed(place, sem):
        remote(place, place, sent.at[0], sem, sibling).wait_recv()

    def settle(event):
        there = z_of(event)
        role = role_of(there)
        rows = rows_of(role)

        @pl.when(role == 0)
        def _():
            landed(units.at[there], us_r.at[there])
            gall[there, y, core, EXTRA] = (
                part[there, core, EXTRA] + units[there, 3] + units[there, 4] + units[there, 5]
            ).astype(BF16)
            for d in (2, 1, 3):
                extra_tile_copy(there, d).start()

        @pl.when(role != 0)
        def _():
            landed(units.at[there, pl.ds(0, 3)], us_r.at[there])

        gall[there, y, core, rows] = (
            part[there, core, rows] + units[there, 0] + units[there, 1] + units[there, 2]
        ).astype(BF16)
        for d in (2, 1, 3):
            tile_copy(there, d).start()

    def share(there, k, core_):
        place = gall.at[there, wrap(y + k, Y), core_]
        return remote(place, place, sent.at[7], gs_r.at[there], sibling)

    def spread(event):
        there = z_of(event)
        role = role_of(there)
        @pl.when(role == 0)
        def _():
            landed(gall.at[there, y, core, pl.ds(0, 3 * UNIT)], gt_r.at[there])

        @pl.when(role != 0)
        def _():
            landed(gall.at[there, y, core, pl.ds(0, 4 * UNIT)], gt_r.at[there])

        gy[event].start()
        share(there, 0, core).start()

        @pl.when(role == 0)
        def _():
            half = lax.div(there, X)
            gj[z, half] = gall[there, y, core]
            panel_start(half, 0 if event < 4 else 1)

    def meet(event):
        gy[event].recv(0, 0)
        gy[event].recv(1, 0)
        share(z_of(event), 1, core).start()
        share(z_of(event), 3, core).start()

    def close(event):
        gy[event].recv(0, 1)
        share(z_of(event), 2, core).start()

    def multiply(event):
        there = z_of(event)
        landed(gall.at[there, :, other], gs_r.at[there])
        square[...] += jnp.dot(
            gj[there].reshape(ROWS, WIDE), gall[there].reshape(WIDE, WIDE), preferred_element_type=F32
        )

    def first(ring, step):
        ring.recv(0, step)

    def second(ring, step):
        ring.recv(1, step)

    def small(refs, slot, index, device):
        return remote(refs.at[slot], refs.at[slot], sent.at[10 + index], ss_r.at[index], device)

    square[...] = jnp.zeros_like(square)
    first(zr, 0)
    first(yr, 0)
    second(zr, 0)
    second(yr, 0)
    first(zr, 1)
    first(yr, 1)
    form(0)
    form(1)
    join(0)
    form(2)
    join(1)
    join(2)
    second(zr, 1)
    form(3)
    form(4)
    settle(0)
    join(3)
    first(zr, 2)
    settle(1)
    settle(2)
    join(4)
    second(zr, 2)
    spread(0)
    form(5)
    form(6)
    spread(1)
    join(5)
    settle(3)
    spread(2)
    join(6)
    first(zr, 3)
    form(7)
    settle(4)
    join(7)

    total = ss_z[0]
    for k in range(1, Z):
        total = total + ss_z[k]
    ss_y[y] = total
    for d in (1, 2, 3):
        small(ss_y, y, 0, at_y(wrap(y + d, Y))).start()

    meet(0)
    meet(1)
    spread(3)
    settle(5)
    meet(2)
    settle(6)
    spread(4)
    panel_on(False)
    settle(7)
    spread(5)
    meet(3)
    spread(6)
    spread(7)
    meet(4)

    landed(ss_y.at[pl.ds(0, 3)], ss_r.at[0])
    ss_x[x] = ss_y[0] + ss_y[1] + ss_y[2] + ss_y[3]
    for d in (1, 2, 3):
        small(ss_x, x, 1, at_x(wrap(x + d, X))).start()

    close(0)
    close(1)
    close(2)
    meet(5)
    panel_on(True)
    meet(6)
    meet(7)

    landed(ss_x.at[pl.ds(0, 3)], ss_r.at[1])
    ss_c[core] = ss_x[0] + ss_x[1] + ss_x[2] + ss_x[3]
    small(ss_c, core, 2, sibling).start()

    close(3)
    close(4)
    multiply(0)
    close(5)
    panel_wait(1)
    multiply(1)
    multiply(2)
    close(6)
    multiply(3)
    close(7)
    multiply(4)
    small(ss_c, other, 2, sibling).wait_recv()
    norm_total = (ss_c[0] + ss_c[1])[0:1, 0:1]
    factor = math.sqrt(FULL_ROWS) / (3.0 * (jnp.sqrt(norm_total) + norm_eps))
    factor_out[...] = jnp.broadcast_to(math.sqrt(FULL_COLS) * factor, factor_out.shape)
    panel_wait(3)
    multiply(5)
    multiply(6)
    panel_wait(4)
    multiply(7)

    pr = Ring(X, x, at_x, lambda b, p: pb.at[p, b, core], pb.at[:, 0, core], sent.at[8], pr_r)
    for half in (0, 1):
        gram = gj[z, half].astype(F32)
        tile = (
            cubic_coef * factor * factor * gram
            + quintic_coef * (factor * factor) * (factor * factor) * square[pl.ds(half * HALF, HALF)]
        )
        pb[half, x, core] = tile.astype(BF16)
    pr.start()

    def share_p(index, core_):
        place = pb.at[:, wrap(x + index, X), core_]
        return remote(place, place, sent.at[9], ps_r.at[index], sibling)

    def y_relay_copy(tile, side):
        return remote(
            up.at[tile, wrap(y + 2, Y), pl.ds(side * HALF, HALF)],
            y_relay.at[tile, side],
            sent.at[13],
            ur_r.at[tile],
            at_y(wrap(y + 1 - 2 * side, Y)),
        )

    def y_last_copy(tile, side, half):
        return remote(
            up.at[tile, wrap(y + 1 - 2 * side, Y), pl.ds(half * HALF, HALF)],
            y_last.at[tile, side, pl.ds(half * HALF, HALF)],
            sent.at[14],
            ul_r.at[tile],
            at_y(wrap(y + 1 - 2 * side, Y)),
        )

    def add_relay(tile):
        landed(y_relay.at[tile], ur_r.at[tile])
        for side in (0, 1):
            near = wrap(y + 1 - 2 * side, Y)
            place = pl.ds(side * HALF, HALF)
            up[tile, near, place] = up[tile, near, place] + y_relay[tile, side]
            y_last_copy(tile, side, side).start()

    def z_sum_copy(way, step, half):
        sign = 1 - 2 * way
        return remote(
            uz.at[wrap(z + sign * (4 - step), Z), pl.ds(half * HALF, HALF)],
            z_sum.at[way, step, half],
            sent.at[15],
            zs_r.at[2 * step + (half + way) % 2],
            at_z(wrap(z + sign, Z)),
        )

    def z_sum_step(step, second_half):
        landed(z_sum.at[0, 0], zs_r.at[2 * step + second_half])
        for way in (0, 1):
            half = way if not second_half else 1 - way
            near = wrap(z + (1 - 2 * way) * (3 - step), Z)
            place = pl.ds(half * HALF, HALF)
            uz[near, place] = uz[near, place] + z_sum[way, step, half]
            z_sum_copy(way, step + 1, half).start()

    def grow(index):
        there = wrap(x + index, X)
        landed(pb.at[:, there, other], ps_r.at[index])
        for half in (0, 1):
            uz[there + half * X] = jnp.dot(
                pb[half, there].reshape(ROWS, WIDE),
                xa[:, :, pl.ds(SPLIT, TILE)].reshape(WIDE, TILE),
                preferred_element_type=F32,
            )
        if index == 2:
            for way in (0, 1):
                z_sum_copy(way, 0, way).start()
            for way in (0, 1):
                z_sum_copy(way, 1, 1 - way).start()
        for tile in range(TILES):
            columns = pl.ds(tile * TILE, TILE)
            term = lax.dot_general(
                pb[:, there].reshape(2 * ROWS, WIDE),
                jnp.concatenate([xb[there, :, columns], xb[there + X, :, columns]], axis=0),
                TN,
                preferred_element_type=F32,
            ).reshape(Y, ROWS, TILE)
            up[tile] = term if index == 0 else up[tile] + term
            if index == 2:
                for side in (0, 1):
                    y_relay_copy(tile, side).start()

    def begin_near(tile):
        for side in (0, 1):
            y_last_copy(tile, side, 1 - side).start()

    def finish_y(tile):
        landed(y_last.at[tile], ul_r.at[tile])
        columns = pl.ds(tile * TILE, TILE)
        product[:, columns] = (
            linear_coef * xb[z, :, columns].astype(F32) + up[tile, y] + y_last[tile, 0] + y_last[tile, 1]
        )

    def finish_z(half):
        if half == 0:
            landed(z_sum.at[0, 0], zs_r.at[6])
            landed(z_sum.at[0, 0], zs_r.at[7])
        rows, columns = pl.ds(half * HALF, HALF), pl.ds(SPLIT, TILE)
        product[rows, columns] = (
            linear_coef * xb[z, rows, columns].astype(F32)
            + uz[z, rows]
            + z_sum[0, 3, half]
            + z_sum[1, 3, half]
        )

    share_p(0, core).start()
    grow(0)
    first(pr, 0)
    second(pr, 0)
    share_p(1, core).start()
    share_p(3, core).start()
    grow(1)
    first(pr, 1)
    share_p(2, core).start()
    grow(3)
    grow(2)
    begin_near(0)
    begin_near(1)
    z_sum_step(0, False)
    add_relay(0)
    z_sum_step(1, True)
    add_relay(1)
    z_sum_step(1, False)
    z_sum_step(2, True)
    z_sum_step(2, False)
    finish_y(0)
    finish_y(1)
    finish_z(0)
    finish_z(1)

    for index, place in enumerate((
        xb.at[pl.ds(0, 7)],
        xa.at[pl.ds(0, 3)],
        part.at[:, 0],
        units.at[pl.ds(0, 5)],
        gj.at[pl.ds(0, 7)],
        gall.at[pl.ds(0, 3), pl.ds(0, 2), 0],
        gall.at[:, pl.ds(0, 3), 0],
        gall.at[:, :, 0],
        pb.at[0, pl.ds(0, 3)],
        pb.at[:, :, 0],
        ss_y.at[pl.ds(0, 3)],
        ss_x.at[pl.ds(0, 3)],
        ss_c.at[0],
        y_relay,
        y_last,
        uz.at[pl.ds(0, 7)],
    )):
        remote(place, place, sent.at[index], zr_r.at[0], sibling).wait_send()


def dma(*shape):
    return pltpu.SemaphoreType.DMA(shape)


def fused(momentum, gradient):
    vmem = pl.BlockSpec(memory_space=pltpu.VMEM)
    return pl.pallas_call(
        kernel,
        out_shape=(
            jax.ShapeDtypeStruct((ROWS, COLS), F32),
            jax.ShapeDtypeStruct((8, COLS), F32),
        ),
        in_specs=[pl.BlockSpec(memory_space=pl.ANY)] * 2,
        out_specs=(vmem, vmem),
        scratch_shapes=[
            pltpu.VMEM((ROWS, COLS), F32),
            pltpu.VMEM((ROWS, COLS), BF16),
            dma(2),
            pltpu.VMEM((Y, ROWS, COLS), BF16),
            pltpu.VMEM((Z, ROWS, COLS), BF16),
            pltpu.VMEM((Z, 2, HALF, WIDE), F32),
            pltpu.VMEM((Z, HALF, WIDE), F32),
            pltpu.VMEM((Z, 6, UNIT, WIDE), F32),
            pltpu.VMEM((Z, 2, HALF, WIDE), BF16),
            pltpu.VMEM((Z, Y, 2, HALF, WIDE), BF16),
            pltpu.VMEM((2, X, 2, HALF, WIDE), BF16),
            pltpu.VMEM((TILES, Y, ROWS, TILE), F32),
            pltpu.VMEM((TILES, 2, HALF, TILE), F32),
            pltpu.VMEM((TILES, 2, ROWS, TILE), F32),
            pltpu.VMEM((Z, ROWS, TILE), F32),
            pltpu.VMEM((2, 4, 2, HALF, TILE), F32),
            pltpu.VMEM((ROWS, WIDE), F32),
            pltpu.VMEM((Z, 8, 128), F32),
            pltpu.VMEM((Y, 8, 128), F32),
            pltpu.VMEM((X, 8, 128), F32),
            pltpu.VMEM((2, 8, 128), F32),
            dma(16),
            dma(7),
            dma(3),
            dma(Z),
            dma(Z),
            dma(8),
            dma(Z),
            dma(Z, 3),
            dma(Z),
            dma(3),
            dma(X),
            dma(3),
            dma(TILES),
            dma(TILES),
            dma(8),
        ],
        compiler_params=pltpu.CompilerParams(
            collective_id=0, has_side_effects=True, vmem_limit_bytes=56 * 1024 * 1024
        ),
    )(momentum, gradient)


def local(momentum, gradient):
    new_momentum = decay_rate * momentum + gradient.astype(F32)
    product, scale = fused(momentum, gradient)
    update = (scale * product.reshape(ROWS // 8, 8, COLS)).reshape(ROWS, COLS)
    return (new_momentum, update)


def solution(mesh):
    placed = (P("row", "col"), P("row", "col"))
    return jax.shard_map(
        local,
        mesh=mesh,
        in_specs=placed,
        out_specs=(P("row", "col"), P("row", "col")),
        check_vma=False,
    )
```

```python
import math

import jax
import jax.numpy as jnp
from jax import lax
from jax.experimental import pallas as pl
from jax.experimental.pallas import tpu as pltpu
from jax.sharding import PartitionSpec as P

decay_rate = 0.95
linear_coef = 3.4445
cubic_coef = -4.775
quintic_coef = 2.0315
norm_eps = 1e-07

X, Y, Z = 4, 4, 8
ROWS, COLS = 160, 1152
HALF = ROWS // 2
WIDE = Y * ROWS
UNIT = 16
EXTRA = pl.ds(UNIT, UNIT)
TILES = 2
TILE = COLS // 3
SPLIT = TILES * TILE
FULL_ROWS = ROWS * Y * Z
FULL_COLS = COLS * X * 2
NT = (((1,), (1,)), ((), ()))
TN = (((0,), (0,)), ((), ()))
F32 = jnp.float32
BF16 = jnp.bfloat16


def wrap(value, size):
    return lax.rem(value + size, size)


def remote(src, dst, send_sem, recv_sem, device):
    return pltpu.make_async_remote_copy(
        src_ref=src,
        dst_ref=dst,
        send_sem=send_sem,
        recv_sem=recv_sem,
        device_id=device,
        device_id_type=pl.DeviceIdType.MESH,
    )


class Ring:
    def __init__(self, size, position, device, region, whole, send_sem, recv_sems):
        self.size, self.position, self.device = size, position, device
        self.region, self.whole = region, whole
        self.send_sem, self.recv_sems = send_sem, recv_sems

    def send(self, kind, step):
        for way in (0, 1):
            sign = 1 - 2 * way
            place = self.region(
                wrap(self.position - sign * step, self.size), way if kind == 0 else 1 - way
            )
            remote(
                place,
                place,
                self.send_sem,
                self.recv_sems.at[2 * step + kind],
                self.device(wrap(self.position + sign, self.size)),
            ).start()

    def start(self):
        self.send(0, 0)
        self.send(1, 0)

    def recv(self, kind, step):
        remote(
            self.whole, self.whole, self.send_sem, self.recv_sems.at[2 * step + kind], self.device(self.position)
        ).wait_recv()
        if step + 1 < self.size // 2 - kind:
            self.send(kind, step + 1)


OFFSETS = (0, 1, -1, 2, -2, 3, -3, 4)


def kernel(
    momentum,
    gradient,
    update,
    momentum_here, gradient_here, load_sems, xa, xb, part, sibling_part, units, gj, gall, pb, up, y_relay, y_last, uz, z_sum,
    square, ss_z, ss_y, ss_x, ss_c,
    sent, zr_r, yr_r, sp_r, us_r, gz_r, gt_r, gy_r, gs_r, pr_r, ps_r, ss_r, ur_r, ul_r, zs_r,
):
    row, col = lax.axis_index("row"), lax.axis_index("col")
    z, y = lax.div(row, Y), lax.rem(row, Y)
    x, core = lax.div(col, 2), lax.rem(col, 2)
    other = 1 - core

    def at_z(p):
        return (p * Y + y, col)

    def at_y(p):
        return (z * Y + p, col)

    def at_x(p):
        return (row, p * 2 + core)

    sibling = (row, x * 2 + other)

    barrier = pltpu.get_barrier_semaphore()
    partners = [at_z(wrap(z + d, Z)) for d in (1, -1, 2, -2)] + [sibling]
    partners += [at_y(wrap(y + d, Y)) for d in (1, 2, 3)]
    partners += [at_x(wrap(x + d, X)) for d in (1, 2, 3)]
    for partner in partners:
        pl.semaphore_signal(barrier, inc=1, device_id=partner, device_id_type=pl.DeviceIdType.MESH)
    loads = [
        pltpu.make_async_copy(momentum, momentum_here, load_sems.at[0]),
        pltpu.make_async_copy(gradient, gradient_here, load_sems.at[1]),
    ]
    for copy in loads:
        copy.start()
    for copy in loads:
        copy.wait()
    iterate = (decay_rate * momentum_here[...] + gradient_here[...].astype(F32)).astype(BF16)
    xb[z] = iterate
    xa[y] = iterate
    pl.semaphore_wait(barrier, len(partners))

    zr = Ring(Z, z, at_z, lambda b, p: xb.at[b, pl.ds(p * HALF, HALF)], xb.at[0], sent.at[0], zr_r)
    yr = Ring(Y, y, at_y, lambda b, p: xa.at[b, pl.ds(p * HALF, HALF)], xa.at[0], sent.at[1], yr_r)
    for kind in (0, 1):
        zr.send(kind, 0)
        yr.send(kind, 0)

    def z_of(event):
        return wrap(z + OFFSETS[event], Z)

    def sibling_copy(there):
        return remote(
            part.at[there, other], sibling_part.at[there], sent.at[2], sp_r.at[there], sibling
        )

    def form(event):
        there = z_of(event)
        block = xb[there]
        part[there] = lax.dot_general(
            block, xa[...].reshape(WIDE, COLS), NT, preferred_element_type=F32
        ).reshape(2, HALF, WIDE)
        sibling_copy(there).start()
        wide = block.astype(F32)
        ss_z[there] = jnp.broadcast_to(jnp.sum(wide * wide, keepdims=True), (8, 128))

    def role_of(there):
        return wrap(x - lax.rem(there, X), X)

    def rows_of(unit):
        return pl.ds(pl.multiple_of(UNIT * (unit + lax.div(unit + 2, 3)), UNIT), UNIT)

    def unit_copy(there, d):
        to = wrap(x + d, X)
        return remote(
            part.at[there, core, rows_of(wrap(to - lax.rem(there, X), X))],
            units.at[there, d - 1],
            sent.at[3],
            us_r.at[there],
            at_x(to),
        )

    def extra_copy(there, slot):
        return remote(
            part.at[there, core, EXTRA],
            units.at[there, 3 + slot],
            sent.at[3],
            us_r.at[there],
            at_x(lax.rem(there, X)),
        )

    def join(event):
        there = z_of(event)
        sibling_copy(there).wait_recv()
        part[there, core] = part[there, core] + sibling_part[there]
        for d in (1, 3, 2):
            unit_copy(there, d).start()
        role = role_of(there)

        @pl.when(role != 0)
        def _():
            extra_copy(there, 3 - role).start()

    cut = ((0, 48), (48, 32))
    def panel_copy(way, hops, block, slot, piece):
        place = gj.at[block, piece]
        return remote(
            place, place, sent.at[4], gz_r.at[slot], at_z(wrap(z + (1 - 2 * way) * hops, Z))
        )

    def panel_start(piece, late):
        for hops in (2, 1):
            for way in (0, 1):
                slot = 0 if hops == 1 else 4 + 2 * way + late
                panel_copy(way, hops, z, slot, piece).start()

    def panel_on(late):
        for way in (0, 1):
            block = wrap(z - (1 - 2 * way) * 2, Z)
            near = lax.div(wrap(wrap(x - block, Z) + 1 - Z, Z), X)
            middle = wrap(wrap(x - block, Z) - Z, X) == 2

            def go(piece, slot):
                landed(gj.at[0, 0], gz_r.at[slot])

                @pl.when(piece == way)
                def _():
                    panel_copy(way, 2, block, 3, piece).start()

                panel_copy(way, 1, block, 2, piece).start()

            @pl.when(middle if late else jnp.logical_not(middle))
            def _():
                go(near, 4 + 2 * way)

            if late:
                go(1 - near, 5 + 2 * way)

    def panel_wait(distance):
        landed(gj.at[pl.ds(0, 2)] if distance < 4 else gj.at[0], gz_r.at[distance - 1])

    gy = []
    for event in range(Z):
        there = z_of(event)
        gy.append(
            Ring(
                Y,
                y,
                at_y,
                lambda b, p, there=there: gall.at[there, b, core, pl.ds(*cut[p])],
                gall.at[there, 0, core],
                sent.at[6],
                gy_r.at[there],
            )
        )

    def tile_copy(there, d):
        place = gall.at[there, y, core, rows_of(role_of(there))]
        return remote(place, place, sent.at[5], gt_r.at[there], at_x(wrap(x + d, X)))

    def extra_tile_copy(there, d):
        place = gall.at[there, y, core, EXTRA]
        return remote(place, place, sent.at[5], gt_r.at[there], at_x(wrap(x + d, X)))

    def landed(place, sem):
        remote(place, place, sent.at[0], sem, sibling).wait_recv()

    def settle(event):
        there = z_of(event)
        role = role_of(there)
        rows = rows_of(role)

        @pl.when(role == 0)
        def _():
            landed(units.at[there], us_r.at[there])
            gall[there, y, core, EXTRA] = (
                part[there, core, EXTRA] + units[there, 3] + units[there, 4] + units[there, 5]
            ).astype(BF16)
            for d in (1, 3, 2):
                extra_tile_copy(there, d).start()

        @pl.when(role != 0)
        def _():
            landed(units.at[there, pl.ds(0, 3)], us_r.at[there])

        gall[there, y, core, rows] = (
            part[there, core, rows] + units[there, 0] + units[there, 1] + units[there, 2]
        ).astype(BF16)
        for d in (1, 3, 2):
            tile_copy(there, d).start()

    def share(there, k, core_):
        place = gall.at[there, wrap(y + k, Y), core_]
        return remote(place, place, sent.at[7], gs_r.at[there], sibling)

    def spread(event):
        there = z_of(event)
        role = role_of(there)
        @pl.when(role == 0)
        def _():
            landed(gall.at[there, y, core, pl.ds(0, 3 * UNIT)], gt_r.at[there])

        @pl.when(role != 0)
        def _():
            landed(gall.at[there, y, core, pl.ds(0, 4 * UNIT)], gt_r.at[there])

        gy[event].start()
        share(there, 0, core).start()

        @pl.when(role == 0)
        def _():
            half = lax.div(there, X)
            gj[z, half] = gall[there, y, core]
            panel_start(half, 0 if event < 4 else 1)

    def meet(event):
        gy[event].recv(0, 0)
        gy[event].recv(1, 0)
        share(z_of(event), 1, core).start()
        share(z_of(event), 3, core).start()

    def close(event):
        gy[event].recv(0, 1)
        share(z_of(event), 2, core).start()

    def multiply(event):
        there = z_of(event)
        landed(gall.at[there, :, other], gs_r.at[there])
        square[...] += jnp.dot(
            gj[there].reshape(ROWS, WIDE), gall[there].reshape(WIDE, WIDE), preferred_element_type=F32
        )

    def first(ring, step):
        ring.recv(0, step)

    def second(ring, step):
        ring.recv(1, step)

    def small(refs, slot, index, device):
        return remote(refs.at[slot], refs.at[slot], sent.at[10 + index], ss_r.at[index], device)

    square[...] = jnp.zeros_like(square)
    first(zr, 0)
    first(yr, 0)
    second(zr, 0)
    second(yr, 0)
    first(zr, 1)
    first(yr, 1)
    form(0)
    form(1)
    join(0)
    form(2)
    join(1)
    second(zr, 1)
    join(2)
    form(3)
    form(4)
    settle(0)
    join(3)
    first(zr, 2)
    settle(1)
    settle(2)
    join(4)
    second(zr, 2)
    spread(0)
    form(5)
    form(6)
    spread(1)
    join(5)
    settle(3)
    spread(2)
    join(6)
    first(zr, 3)
    form(7)
    settle(4)
    join(7)

    total = ss_z[0]
    for k in range(1, Z):
        total = total + ss_z[k]
    ss_y[y] = total
    for d in (1, 2, 3):
        small(ss_y, y, 0, at_y(wrap(y + d, Y))).start()

    meet(0)
    meet(1)
    spread(3)
    settle(5)
    meet(2)
    settle(6)
    spread(4)
    panel_on(False)
    settle(7)
    spread(5)
    meet(3)
    spread(6)
    spread(7)
    meet(4)

    landed(ss_y.at[pl.ds(0, 3)], ss_r.at[0])
    ss_x[x] = ss_y[0] + ss_y[1] + ss_y[2] + ss_y[3]
    for d in (1, 2, 3):
        small(ss_x, x, 1, at_x(wrap(x + d, X))).start()

    close(0)
    close(1)
    close(2)
    meet(5)
    panel_on(True)
    meet(6)
    meet(7)

    landed(ss_x.at[pl.ds(0, 3)], ss_r.at[1])
    ss_c[core] = ss_x[0] + ss_x[1] + ss_x[2] + ss_x[3]
    small(ss_c, core, 2, sibling).start()

    close(3)
    close(4)
    multiply(0)
    close(5)
    panel_wait(1)
    multiply(1)
    multiply(2)
    close(6)
    multiply(3)
    close(7)
    multiply(4)
    small(ss_c, other, 2, sibling).wait_recv()
    norm_total = (ss_c[0] + ss_c[1])[0:1, 0:1]
    factor = math.sqrt(FULL_ROWS) / (3.0 * (jnp.sqrt(norm_total) + norm_eps))
    scale = math.sqrt(FULL_COLS) * factor
    panel_wait(3)
    multiply(5)
    multiply(6)
    panel_wait(4)
    multiply(7)

    pr = Ring(X, x, at_x, lambda b, p: pb.at[p, b, core], pb.at[:, 0, core], sent.at[8], pr_r)
    for half in (0, 1):
        gram = gj[z, half].astype(F32)
        tile = (
            cubic_coef * factor * factor * gram
            + quintic_coef * (factor * factor) * (factor * factor) * square[pl.ds(half * HALF, HALF)]
        )
        pb[half, x, core] = tile.astype(BF16)
    pr.start()

    def share_p(index, core_):
        place = pb.at[:, wrap(x + index, X), core_]
        return remote(place, place, sent.at[9], ps_r.at[index], sibling)

    def y_relay_copy(tile, side):
        return remote(
            up.at[tile, wrap(y + 2, Y), pl.ds(side * HALF, HALF)],
            y_relay.at[tile, side],
            sent.at[13],
            ur_r.at[tile],
            at_y(wrap(y + 1 - 2 * side, Y)),
        )

    def y_last_copy(tile, side, half):
        return remote(
            up.at[tile, wrap(y + 1 - 2 * side, Y), pl.ds(half * HALF, HALF)],
            y_last.at[tile, side, pl.ds(half * HALF, HALF)],
            sent.at[14],
            ul_r.at[tile],
            at_y(wrap(y + 1 - 2 * side, Y)),
        )

    def add_relay(tile):
        landed(y_relay.at[tile], ur_r.at[tile])
        for side in (0, 1):
            near = wrap(y + 1 - 2 * side, Y)
            place = pl.ds(side * HALF, HALF)
            up[tile, near, place] = up[tile, near, place] + y_relay[tile, side]
            y_last_copy(tile, side, side).start()

    def z_sum_copy(way, step, half):
        sign = 1 - 2 * way
        return remote(
            uz.at[wrap(z + sign * (4 - step), Z), pl.ds(half * HALF, HALF)],
            z_sum.at[way, step, half],
            sent.at[15],
            zs_r.at[2 * step + (half + way) % 2],
            at_z(wrap(z + sign, Z)),
        )

    def z_sum_step(step, second_half):
        landed(z_sum.at[0, 0], zs_r.at[2 * step + second_half])
        for way in (0, 1):
            half = way if not second_half else 1 - way
            near = wrap(z + (1 - 2 * way) * (3 - step), Z)
            place = pl.ds(half * HALF, HALF)
            uz[near, place] = uz[near, place] + z_sum[way, step, half]
            z_sum_copy(way, step + 1, half).start()

    def grow(index):
        there = wrap(x + index, X)
        landed(pb.at[:, there, other], ps_r.at[index])
        for half in (0, 1):
            uz[there + half * X] = jnp.dot(
                pb[half, there].reshape(ROWS, WIDE),
                xa[:, :, pl.ds(SPLIT, TILE)].reshape(WIDE, TILE),
                preferred_element_type=F32,
            )
        if index == 2:
            for way in (0, 1):
                z_sum_copy(way, 0, way).start()
            for way in (0, 1):
                z_sum_copy(way, 1, 1 - way).start()
        for tile in range(TILES):
            columns = pl.ds(tile * TILE, TILE)
            term = lax.dot_general(
                pb[:, there].reshape(2 * ROWS, WIDE),
                jnp.concatenate([xb[there, :, columns], xb[there + X, :, columns]], axis=0),
                TN,
                preferred_element_type=F32,
            ).reshape(Y, ROWS, TILE)
            up[tile] = term if index == 0 else up[tile] + term
            if index == 2:
                for side in (0, 1):
                    y_relay_copy(tile, side).start()

    def begin_near(tile):
        for side in (0, 1):
            y_last_copy(tile, side, 1 - side).start()

    def finish_y(tile):
        landed(y_last.at[tile], ul_r.at[tile])
        columns = pl.ds(tile * TILE, TILE)
        update[:, columns] = scale * (
            linear_coef * xb[z, :, columns].astype(F32) + up[tile, y] + y_last[tile, 0] + y_last[tile, 1]
        )

    def finish_z(half):
        if half == 0:
            landed(z_sum.at[0, 0], zs_r.at[6])
            landed(z_sum.at[0, 0], zs_r.at[7])
        rows, columns = pl.ds(half * HALF, HALF), pl.ds(SPLIT, TILE)
        update[rows, columns] = scale * (
            linear_coef * xb[z, rows, columns].astype(F32)
            + uz[z, rows]
            + z_sum[0, 3, half]
            + z_sum[1, 3, half]
        )

    share_p(0, core).start()
    grow(0)
    first(pr, 0)
    second(pr, 0)
    share_p(1, core).start()
    share_p(3, core).start()
    first(pr, 1)
    share_p(2, core).start()
    grow(1)
    grow(3)
    grow(2)
    begin_near(0)
    begin_near(1)
    z_sum_step(0, False)
    add_relay(0)
    z_sum_step(1, True)
    add_relay(1)
    z_sum_step(1, False)
    z_sum_step(2, True)
    z_sum_step(2, False)
    finish_y(0)
    finish_y(1)
    finish_z(0)
    finish_z(1)

    for index, place in enumerate((
        xb.at[pl.ds(0, 7)],
        xa.at[pl.ds(0, 3)],
        part.at[:, 0],
        units.at[pl.ds(0, 5)],
        gj.at[pl.ds(0, 7)],
        gall.at[pl.ds(0, 3), pl.ds(0, 2), 0],
        gall.at[:, pl.ds(0, 3), 0],
        gall.at[:, :, 0],
        pb.at[0, pl.ds(0, 3)],
        pb.at[:, :, 0],
        ss_y.at[pl.ds(0, 3)],
        ss_x.at[pl.ds(0, 3)],
        ss_c.at[0],
        y_relay,
        y_last,
        uz.at[pl.ds(0, 7)],
    )):
        remote(place, place, sent.at[index], zr_r.at[0], sibling).wait_send()


def dma(*shape):
    return pltpu.SemaphoreType.DMA(shape)


def fused(momentum, gradient):
    vmem = pl.BlockSpec(memory_space=pltpu.VMEM)
    return pl.pallas_call(
        kernel,
        out_shape=jax.ShapeDtypeStruct((ROWS, COLS), F32),
        in_specs=[pl.BlockSpec(memory_space=pl.ANY)] * 2,
        out_specs=vmem,
        scratch_shapes=[
            pltpu.VMEM((ROWS, COLS), F32),
            pltpu.VMEM((ROWS, COLS), BF16),
            dma(2),
            pltpu.VMEM((Y, ROWS, COLS), BF16),
            pltpu.VMEM((Z, ROWS, COLS), BF16),
            pltpu.VMEM((Z, 2, HALF, WIDE), F32),
            pltpu.VMEM((Z, HALF, WIDE), F32),
            pltpu.VMEM((Z, 6, UNIT, WIDE), F32),
            pltpu.VMEM((Z, 2, HALF, WIDE), BF16),
            pltpu.VMEM((Z, Y, 2, HALF, WIDE), BF16),
            pltpu.VMEM((2, X, 2, HALF, WIDE), BF16),
            pltpu.VMEM((TILES, Y, ROWS, TILE), F32),
            pltpu.VMEM((TILES, 2, HALF, TILE), F32),
            pltpu.VMEM((TILES, 2, ROWS, TILE), F32),
            pltpu.VMEM((Z, ROWS, TILE), F32),
            pltpu.VMEM((2, 4, 2, HALF, TILE), F32),
            pltpu.VMEM((ROWS, WIDE), F32),
            pltpu.VMEM((Z, 8, 128), F32),
            pltpu.VMEM((Y, 8, 128), F32),
            pltpu.VMEM((X, 8, 128), F32),
            pltpu.VMEM((2, 8, 128), F32),
            dma(16),
            dma(7),
            dma(3),
            dma(Z),
            dma(Z),
            dma(8),
            dma(Z),
            dma(Z, 3),
            dma(Z),
            dma(3),
            dma(X),
            dma(3),
            dma(TILES),
            dma(TILES),
            dma(8),
        ],
        compiler_params=pltpu.CompilerParams(
            collective_id=0, has_side_effects=True, vmem_limit_bytes=56 * 1024 * 1024
        ),
    )(momentum, gradient)


def local(momentum, gradient):
    new_momentum = decay_rate * momentum + gradient.astype(F32)
    update = fused(momentum, gradient)
    return (new_momentum, update)


def solution(mesh):
    placed = (P("row", "col"), P("row", "col"))
    return jax.shard_map(
        local,
        mesh=mesh,
        in_specs=placed,
        out_specs=(P("row", "col"), P("row", "col")),
        check_vma=False,
    )
```

```python
import math

import jax
import jax.numpy as jnp
from jax import lax
from jax.experimental import pallas as pl
from jax.experimental.pallas import tpu as pltpu
from jax.sharding import PartitionSpec as P

decay_rate = 0.95
linear_coef = 3.4445
cubic_coef = -4.775
quintic_coef = 2.0315
norm_eps = 1e-07

X, Y, Z = 4, 4, 8
ROWS, COLS = 160, 1152
HALF = ROWS // 2
WIDE = Y * ROWS
UNIT = 16
EXTRA = pl.ds(UNIT, UNIT)
TILES = 2
TILE = COLS // 3
SPLIT = TILES * TILE
FULL_ROWS = ROWS * Y * Z
FULL_COLS = COLS * X * 2
NT = (((1,), (1,)), ((), ()))
TN = (((0,), (0,)), ((), ()))
F32 = jnp.float32
BF16 = jnp.bfloat16


def wrap(value, size):
    return lax.rem(value + size, size)


def remote(src, dst, send_sem, recv_sem, device):
    return pltpu.make_async_remote_copy(
        src_ref=src,
        dst_ref=dst,
        send_sem=send_sem,
        recv_sem=recv_sem,
        device_id=device,
        device_id_type=pl.DeviceIdType.MESH,
    )


class Ring:
    def __init__(self, size, position, device, region, whole, send_sem, recv_sems):
        self.size, self.position, self.device = size, position, device
        self.region, self.whole = region, whole
        self.send_sem, self.recv_sems = send_sem, recv_sems

    def send(self, kind, step):
        for way in (0, 1):
            sign = 1 - 2 * way
            place = self.region(
                wrap(self.position - sign * step, self.size), way if kind == 0 else 1 - way
            )
            remote(
                place,
                place,
                self.send_sem,
                self.recv_sems.at[2 * step + kind],
                self.device(wrap(self.position + sign, self.size)),
            ).start()

    def start(self):
        self.send(0, 0)
        self.send(1, 0)

    def recv(self, kind, step):
        remote(
            self.whole, self.whole, self.send_sem, self.recv_sems.at[2 * step + kind], self.device(self.position)
        ).wait_recv()
        if step + 1 < self.size // 2 - kind:
            self.send(kind, step + 1)


OFFSETS = (0, 1, -1, 2, -2, 3, -3, 4)


def kernel(
    momentum,
    gradient,
    update,
    momentum_here, gradient_here, load_sems, xa, xb, part, sibling_part, units, gj, gall, pb, up, y_relay, y_last, uz, z_sum,
    square, ss_z, ss_y, ss_x, ss_c,
    sent, zr_r, yr_r, sp_r, us_r, gz_r, gt_r, gy_r, gs_r, pr_r, ps_r, ss_r, ur_r, ul_r, zs_r,
):
    row, col = lax.axis_index("row"), lax.axis_index("col")
    z, y = lax.div(row, Y), lax.rem(row, Y)
    x, core = lax.div(col, 2), lax.rem(col, 2)
    other = 1 - core

    def at_z(p):
        return (p * Y + y, col)

    def at_y(p):
        return (z * Y + p, col)

    def at_x(p):
        return (row, p * 2 + core)

    sibling = (row, x * 2 + other)

    barrier = pltpu.get_barrier_semaphore()
    partners = [at_z(wrap(z + d, Z)) for d in (1, -1, 2, -2)] + [sibling]
    partners += [at_y(wrap(y + d, Y)) for d in (1, 2, 3)]
    partners += [at_x(wrap(x + d, X)) for d in (1, 2, 3)]
    for partner in partners:
        pl.semaphore_signal(barrier, inc=1, device_id=partner, device_id_type=pl.DeviceIdType.MESH)
    loads = [
        pltpu.make_async_copy(momentum, momentum_here, load_sems.at[0]),
        pltpu.make_async_copy(gradient, gradient_here, load_sems.at[1]),
    ]
    for copy in loads:
        copy.start()
    for copy in loads:
        copy.wait()
    iterate = (decay_rate * momentum_here[...] + gradient_here[...].astype(F32)).astype(BF16)
    xb[z] = iterate
    xa[y] = iterate
    pl.semaphore_wait(barrier, len(partners))

    zr = Ring(Z, z, at_z, lambda b, p: xb.at[b, pl.ds(p * HALF, HALF)], xb.at[0], sent.at[0], zr_r)
    yr = Ring(Y, y, at_y, lambda b, p: xa.at[b, pl.ds(p * HALF, HALF)], xa.at[0], sent.at[1], yr_r)
    for kind in (0, 1):
        zr.send(kind, 0)
        yr.send(kind, 0)

    def z_of(event):
        return wrap(z + OFFSETS[event], Z)

    def sibling_copy(there):
        return remote(
            part.at[there, other], sibling_part.at[there], sent.at[2], sp_r.at[there], sibling
        )

    def form(event):
        there = z_of(event)
        block = xb[there]
        part[there] = lax.dot_general(
            block, xa[...].reshape(WIDE, COLS), NT, preferred_element_type=F32
        ).reshape(2, HALF, WIDE)
        sibling_copy(there).start()
        wide = block.astype(F32)
        ss_z[there] = jnp.broadcast_to(jnp.sum(wide * wide, keepdims=True), (8, 128))

    def role_of(there):
        return wrap(x - lax.rem(there, X), X)

    def rows_of(unit):
        return pl.ds(pl.multiple_of(UNIT * (unit + lax.div(unit + 2, 3)), UNIT), UNIT)

    def unit_copy(there, d):
        to = wrap(x + d, X)
        return remote(
            part.at[there, core, rows_of(wrap(to - lax.rem(there, X), X))],
            units.at[there, d - 1],
            sent.at[3],
            us_r.at[there],
            at_x(to),
        )

    def extra_copy(there, slot):
        return remote(
            part.at[there, core, EXTRA],
            units.at[there, 3 + slot],
            sent.at[3],
            us_r.at[there],
            at_x(lax.rem(there, X)),
        )

    def join(event):
        there = z_of(event)
        sibling_copy(there).wait_recv()
        part[there, core] = part[there, core] + sibling_part[there]
        for d in (1, 3, 2):
            unit_copy(there, d).start()
        role = role_of(there)

        @pl.when(role != 0)
        def _():
            extra_copy(there, 3 - role).start()

    cut = ((0, 48), (48, 32))
    def panel_copy(way, hops, block, slot, piece):
        place = gj.at[block, piece]
        return remote(
            place, place, sent.at[4], gz_r.at[slot], at_z(wrap(z + (1 - 2 * way) * hops, Z))
        )

    def panel_start(piece, late):
        for hops in (2, 1):
            for way in (0, 1):
                slot = 0 if hops == 1 else 4 + 2 * way + late
                panel_copy(way, hops, z, slot, piece).start()

    def panel_on(late):
        for way in (0, 1):
            block = wrap(z - (1 - 2 * way) * 2, Z)
            near = lax.div(wrap(wrap(x - block, Z) + 1 - Z, Z), X)

            def go(piece, slot):
                landed(gj.at[0, 0], gz_r.at[slot])

                @pl.when(piece == way)
                def _():
                    panel_copy(way, 2, block, 3, piece).start()

                panel_copy(way, 1, block, 2, piece).start()

            if late:
                go(1 - near, 5 + 2 * way)
            else:
                go(near, 4 + 2 * way)

    def panel_wait(distance):
        landed(gj.at[pl.ds(0, 2)] if distance < 4 else gj.at[0], gz_r.at[distance - 1])

    gy = []
    for event in range(Z):
        there = z_of(event)
        gy.append(
            Ring(
                Y,
                y,
                at_y,
                lambda b, p, there=there: gall.at[there, b, core, pl.ds(*cut[p])],
                gall.at[there, 0, core],
                sent.at[6],
                gy_r.at[there],
            )
        )

    def tile_copy(there, d):
        place = gall.at[there, y, core, rows_of(role_of(there))]
        return remote(place, place, sent.at[5], gt_r.at[there], at_x(wrap(x + d, X)))

    def extra_tile_copy(there, d):
        place = gall.at[there, y, core, EXTRA]
        return remote(place, place, sent.at[5], gt_r.at[there], at_x(wrap(x + d, X)))

    def landed(place, sem):
        remote(place, place, sent.at[0], sem, sibling).wait_recv()

    def settle(event):
        there = z_of(event)
        role = role_of(there)
        rows = rows_of(role)

        @pl.when(role == 0)
        def _():
            landed(units.at[there], us_r.at[there])
            gall[there, y, core, EXTRA] = (
                part[there, core, EXTRA] + units[there, 3] + units[there, 4] + units[there, 5]
            ).astype(BF16)
            for d in (1, 3, 2):
                extra_tile_copy(there, d).start()

        @pl.when(role != 0)
        def _():
            landed(units.at[there, pl.ds(0, 3)], us_r.at[there])

        gall[there, y, core, rows] = (
            part[there, core, rows] + units[there, 0] + units[there, 1] + units[there, 2]
        ).astype(BF16)
        for d in (1, 3, 2):
            tile_copy(there, d).start()

    def share(there, k, core_):
        place = gall.at[there, wrap(y + k, Y), core_]
        return remote(place, place, sent.at[7], gs_r.at[there], sibling)

    def spread(event):
        there = z_of(event)
        role = role_of(there)
        @pl.when(role == 0)
        def _():
            landed(gall.at[there, y, core, pl.ds(0, 3 * UNIT)], gt_r.at[there])

        @pl.when(role != 0)
        def _():
            landed(gall.at[there, y, core, pl.ds(0, 4 * UNIT)], gt_r.at[there])

        gy[event].start()
        share(there, 0, core).start()

        @pl.when(role == 0)
        def _():
            half = lax.div(there, X)
            gj[z, half] = gall[there, y, core]
            panel_start(half, 0 if event < 4 else 1)

    def meet(event):
        gy[event].recv(0, 0)
        gy[event].recv(1, 0)
        share(z_of(event), 1, core).start()
        share(z_of(event), 3, core).start()

    def close(event):
        gy[event].recv(0, 1)
        share(z_of(event), 2, core).start()

    def multiply(event):
        there = z_of(event)
        landed(gall.at[there, :, other], gs_r.at[there])
        square[...] += jnp.dot(
            gj[there].reshape(ROWS, WIDE), gall[there].reshape(WIDE, WIDE), preferred_element_type=F32
        )

    def first(ring, step):
        ring.recv(0, step)

    def second(ring, step):
        ring.recv(1, step)

    def small(refs, slot, index, device):
        return remote(refs.at[slot], refs.at[slot], sent.at[10 + index], ss_r.at[index], device)

    square[...] = jnp.zeros_like(square)
    first(zr, 0)
    first(yr, 0)
    second(zr, 0)
    second(yr, 0)
    first(zr, 1)
    first(yr, 1)
    form(0)
    form(1)
    join(0)
    form(2)
    join(1)
    second(zr, 1)
    join(2)
    form(3)
    form(4)
    settle(0)
    join(3)
    first(zr, 2)
    settle(1)
    settle(2)
    join(4)
    second(zr, 2)
    spread(0)
    form(5)
    form(6)
    spread(1)
    join(5)
    settle(3)
    spread(2)
    join(6)
    first(zr, 3)
    form(7)
    settle(4)
    join(7)

    total = ss_z[0]
    for k in range(1, Z):
        total = total + ss_z[k]
    ss_y[y] = total
    for d in (1, 2, 3):
        small(ss_y, y, 0, at_y(wrap(y + d, Y))).start()

    meet(0)
    meet(1)
    spread(3)
    settle(5)
    meet(2)
    settle(6)
    spread(4)
    panel_on(False)
    settle(7)
    spread(5)
    meet(3)
    spread(6)
    spread(7)
    meet(4)

    landed(ss_y.at[pl.ds(0, 3)], ss_r.at[0])
    ss_x[x] = ss_y[0] + ss_y[1] + ss_y[2] + ss_y[3]
    for d in (1, 2, 3):
        small(ss_x, x, 1, at_x(wrap(x + d, X))).start()

    close(0)
    close(1)
    close(2)
    meet(5)
    panel_on(True)
    meet(6)
    meet(7)

    landed(ss_x.at[pl.ds(0, 3)], ss_r.at[1])
    ss_c[core] = ss_x[0] + ss_x[1] + ss_x[2] + ss_x[3]
    small(ss_c, core, 2, sibling).start()

    close(3)
    close(4)
    multiply(0)
    close(5)
    panel_wait(1)
    multiply(1)
    multiply(2)
    close(6)
    multiply(3)
    close(7)
    multiply(4)
    small(ss_c, other, 2, sibling).wait_recv()
    norm_total = (ss_c[0] + ss_c[1])[0:1, 0:1]
    factor = math.sqrt(FULL_ROWS) / (3.0 * (jnp.sqrt(norm_total) + norm_eps))
    scale = math.sqrt(FULL_COLS) * factor
    panel_wait(3)
    multiply(5)
    multiply(6)
    panel_wait(4)
    multiply(7)

    pr = Ring(X, x, at_x, lambda b, p: pb.at[p, b, core], pb.at[:, 0, core], sent.at[8], pr_r)
    for half in (0, 1):
        gram = gj[z, half].astype(F32)
        tile = (
            cubic_coef * factor * factor * gram
            + quintic_coef * (factor * factor) * (factor * factor) * square[pl.ds(half * HALF, HALF)]
        )
        pb[half, x, core] = tile.astype(BF16)
    pr.start()

    def share_p(index, core_):
        place = pb.at[:, wrap(x + index, X), core_]
        return remote(place, place, sent.at[9], ps_r.at[index], sibling)

    def y_relay_copy(tile, side):
        return remote(
            up.at[tile, wrap(y + 2, Y), pl.ds(side * HALF, HALF)],
            y_relay.at[tile, side],
            sent.at[13],
            ur_r.at[tile],
            at_y(wrap(y + 1 - 2 * side, Y)),
        )

    def y_last_copy(tile, side, half):
        return remote(
            up.at[tile, wrap(y + 1 - 2 * side, Y), pl.ds(half * HALF, HALF)],
            y_last.at[tile, side, pl.ds(half * HALF, HALF)],
            sent.at[14],
            ul_r.at[tile],
            at_y(wrap(y + 1 - 2 * side, Y)),
        )

    def add_relay(tile):
        landed(y_relay.at[tile], ur_r.at[tile])
        for side in (0, 1):
            near = wrap(y + 1 - 2 * side, Y)
            place = pl.ds(side * HALF, HALF)
            up[tile, near, place] = up[tile, near, place] + y_relay[tile, side]
            y_last_copy(tile, side, side).start()

    def z_sum_copy(way, step, half):
        sign = 1 - 2 * way
        return remote(
            uz.at[wrap(z + sign * (4 - step), Z), pl.ds(half * HALF, HALF)],
            z_sum.at[way, step, half],
            sent.at[15],
            zs_r.at[2 * step + (half + way) % 2],
            at_z(wrap(z + sign, Z)),
        )

    def z_sum_step(step, second_half):
        landed(z_sum.at[0, 0], zs_r.at[2 * step + second_half])
        for way in (0, 1):
            half = way if not second_half else 1 - way
            near = wrap(z + (1 - 2 * way) * (3 - step), Z)
            place = pl.ds(half * HALF, HALF)
            uz[near, place] = uz[near, place] + z_sum[way, step, half]
            z_sum_copy(way, step + 1, half).start()

    def grow(index):
        there = wrap(x + index, X)
        landed(pb.at[:, there, other], ps_r.at[index])
        for half in (0, 1):
            uz[there + half * X] = jnp.dot(
                pb[half, there].reshape(ROWS, WIDE),
                xa[:, :, pl.ds(SPLIT, TILE)].reshape(WIDE, TILE),
                preferred_element_type=F32,
            )
        if index == 2:
            for way in (0, 1):
                z_sum_copy(way, 0, way).start()
            for way in (0, 1):
                z_sum_copy(way, 1, 1 - way).start()
        for tile in range(TILES):
            columns = pl.ds(tile * TILE, TILE)
            term = lax.dot_general(
                pb[:, there].reshape(2 * ROWS, WIDE),
                jnp.concatenate([xb[there, :, columns], xb[there + X, :, columns]], axis=0),
                TN,
                preferred_element_type=F32,
            ).reshape(Y, ROWS, TILE)
            up[tile] = term if index == 0 else up[tile] + term
            if index == 2:
                for side in (0, 1):
                    y_relay_copy(tile, side).start()

    def begin_near(tile):
        for side in (0, 1):
            y_last_copy(tile, side, 1 - side).start()

    def finish_y(tile):
        landed(y_last.at[tile], ul_r.at[tile])
        columns = pl.ds(tile * TILE, TILE)
        update[:, columns] = scale * (
            linear_coef * xb[z, :, columns].astype(F32) + up[tile, y] + y_last[tile, 0] + y_last[tile, 1]
        )

    def finish_z(half):
        if half == 0:
            landed(z_sum.at[0, 0], zs_r.at[6])
            landed(z_sum.at[0, 0], zs_r.at[7])
        rows, columns = pl.ds(half * HALF, HALF), pl.ds(SPLIT, TILE)
        update[rows, columns] = scale * (
            linear_coef * xb[z, rows, columns].astype(F32)
            + uz[z, rows]
            + z_sum[0, 3, half]
            + z_sum[1, 3, half]
        )

    share_p(0, core).start()
    grow(0)
    first(pr, 0)
    second(pr, 0)
    share_p(1, core).start()
    share_p(3, core).start()
    first(pr, 1)
    share_p(2, core).start()
    grow(1)
    grow(3)
    grow(2)
    begin_near(0)
    begin_near(1)
    z_sum_step(0, False)
    add_relay(0)
    z_sum_step(1, True)
    add_relay(1)
    z_sum_step(1, False)
    z_sum_step(2, True)
    z_sum_step(2, False)
    finish_y(0)
    finish_y(1)
    finish_z(0)
    finish_z(1)

    for index, place in enumerate((
        xb.at[pl.ds(0, 7)],
        xa.at[pl.ds(0, 3)],
        part.at[:, 0],
        units.at[pl.ds(0, 5)],
        gj.at[pl.ds(0, 7)],
        gall.at[pl.ds(0, 3), pl.ds(0, 2), 0],
        gall.at[:, pl.ds(0, 3), 0],
        gall.at[:, :, 0],
        pb.at[0, pl.ds(0, 3)],
        pb.at[:, :, 0],
        ss_y.at[pl.ds(0, 3)],
        ss_x.at[pl.ds(0, 3)],
        ss_c.at[0],
        y_relay,
        y_last,
        uz.at[pl.ds(0, 7)],
    )):
        remote(place, place, sent.at[index], zr_r.at[0], sibling).wait_send()


def dma(*shape):
    return pltpu.SemaphoreType.DMA(shape)


def fused(momentum, gradient):
    vmem = pl.BlockSpec(memory_space=pltpu.VMEM)
    return pl.pallas_call(
        kernel,
        out_shape=jax.ShapeDtypeStruct((ROWS, COLS), F32),
        in_specs=[pl.BlockSpec(memory_space=pl.ANY)] * 2,
        out_specs=vmem,
        scratch_shapes=[
            pltpu.VMEM((ROWS, COLS), F32),
            pltpu.VMEM((ROWS, COLS), BF16),
            dma(2),
            pltpu.VMEM((Y, ROWS, COLS), BF16),
            pltpu.VMEM((Z, ROWS, COLS), BF16),
            pltpu.VMEM((Z, 2, HALF, WIDE), F32),
            pltpu.VMEM((Z, HALF, WIDE), F32),
            pltpu.VMEM((Z, 6, UNIT, WIDE), F32),
            pltpu.VMEM((Z, 2, HALF, WIDE), BF16),
            pltpu.VMEM((Z, Y, 2, HALF, WIDE), BF16),
            pltpu.VMEM((2, X, 2, HALF, WIDE), BF16),
            pltpu.VMEM((TILES, Y, ROWS, TILE), F32),
            pltpu.VMEM((TILES, 2, HALF, TILE), F32),
            pltpu.VMEM((TILES, 2, ROWS, TILE), F32),
            pltpu.VMEM((Z, ROWS, TILE), F32),
            pltpu.VMEM((2, 4, 2, HALF, TILE), F32),
            pltpu.VMEM((ROWS, WIDE), F32),
            pltpu.VMEM((Z, 8, 128), F32),
            pltpu.VMEM((Y, 8, 128), F32),
            pltpu.VMEM((X, 8, 128), F32),
            pltpu.VMEM((2, 8, 128), F32),
            dma(16),
            dma(7),
            dma(3),
            dma(Z),
            dma(Z),
            dma(8),
            dma(Z),
            dma(Z, 3),
            dma(Z),
            dma(3),
            dma(X),
            dma(3),
            dma(TILES),
            dma(TILES),
            dma(8),
        ],
        compiler_params=pltpu.CompilerParams(
            collective_id=0, has_side_effects=True, vmem_limit_bytes=56 * 1024 * 1024
        ),
    )(momentum, gradient)


def local(momentum, gradient):
    new_momentum = decay_rate * momentum + gradient.astype(F32)
    update = fused(momentum, gradient)
    return (new_momentum, update)


def solution(mesh):
    placed = (P("row", "col"), P("row", "col"))
    return jax.shard_map(
        local,
        mesh=mesh,
        in_specs=placed,
        out_specs=(P("row", "col"), P("row", "col")),
        check_vma=False,
    )
```
